256 devices in a mesh: tier: 4 (over y_hi, core), grp: 64 (over y_lo, z, x).
Axes of the slice: x: 4, y: 4 (y_hi: 2, y_lo: 2; y = y_hi * 2 + y_lo), z: 8, core: 2. Of those that a mesh axis runs over, the one named last changes fastest.
Arguments:
- resid: bfloat16 [256, 8192], P(('tier', 'grp')), may hold values from -1.5 to 1.5
- query: bfloat16 [256, 8192], P('tier', 'grp'), may hold values from -9 to 9
- fresh_kv: bfloat16 [256, 2048], P('tier', 'grp'), may hold values from -9 to 9
- cache_home: int32 [4, 64], P('tier'), may hold values from 0 to 63, each once within a row
- kv_cache: bfloat16 [256, 128, 2048], P(('tier', 'grp')), may hold values from -9 to 9
- cached_len: int32 [256], P(('tier', 'grp')), may hold values from 1 to 128, 16384 in all
- wo: bfloat16 [8192, 8192], P('grp'), may hold values from -0.0625 to 0.0625
- norm_gain: bfloat16 [8192], replicated, may hold values from 0.099609375 to 1.8984375
- w_router: bfloat16 [8192, 4], replicated, may hold values from -0.0625 to 0.0625
- expert_ids: int32 [256, 2], P(('tier', 'grp')), may hold values from 0 to 3, all different within a row; in each aligned block of 64 rows (0 to 63, 64 to 127, ...) at most 48 rows name the same one
- w_gate: bfloat16 [4, 12288, 8192], P('tier', 'grp'), may hold values from -0.0625 to 0.0625
- w_up: bfloat16 [4, 12288, 8192], P('tier', 'grp'), may hold values from -0.0625 to 0.0625
- w_down: bfloat16 [4, 12288, 8192], P('tier', 'grp'), may hold values from -0.0546875 to 0.0546875
Outputs:
- layer_out: bfloat16 [256, 8192], P(('tier', 'grp'))
The draws below stay inside these ranges and needn't reach their ends.
Inputs may be any that keep to these rules, and one draw needn't show every extreme that they name: Each row of cache_home is a permutation of 0 .. 63. `expert_ids`: the two experts of a row differ; within the rows of one micro-batch (aligned blocks of 64 rows) no expert is named by more than 48 rows, a bound that some block reaches.
All inputs are finite; a program needn't handle non-finite values. No bound on the sum of `cached_len` on one device may be relied on, other than what follows from the above.
Results may differ from the reference program's by a relative error of at most 0.017.
Values may be sent and summed in bfloat16 or wider, within the bound.
A program may use at most 128 MiB of HBM per device.

```python
import math
import jax
import jax.numpy as jnp
import numpy as np
from jax import lax

D = 8192
H = 64
G = 8
HD = 128
FF = 12288
CTX = 128
EXPERTS = 4
BATCH = 64
REQUESTS = 256
CAP = 48
N_TIER = 4


def draw_query(key, part):
    key = jax.random.fold_in(key, 11)
    drawn_draw = jnp.clip(jax.random.normal(key, (REQUESTS, H * HD), jnp.float32), -5.0, 5.0)
    return drawn_draw.astype(jnp.bfloat16)


def draw_fresh_kv(key, part):
    key = jax.random.fold_in(key, 12)
    drawn_draw = jnp.clip(jax.random.normal(key, (REQUESTS, 2 * G * HD), jnp.float32), -5.0, 5.0)
    return drawn_draw.astype(jnp.bfloat16)


def draw_kv_cache(key, part):
    key = jax.random.fold_in(key, 13)
    drawn_draw = jnp.clip(jax.random.normal(key, (REQUESTS, CTX, 2 * G * HD), jnp.float32), -5.0, 5.0)
    return drawn_draw.astype(jnp.bfloat16)


def shard_levels(rng, shape, shards, smallest, top_value):
    loudness = 1.0
    for axis_at, shards_of in shards:
        steps = jax.random.uniform(jax.random.fold_in(jax.random.fold_in(rng, 6), axis_at), (shards_of,), jnp.float32, smallest / len(shards), top_value / len(shards))
        loudness = loudness * jnp.repeat(jnp.exp(steps), shape[axis_at] // shards_of).reshape((-1,) + (1,) * (len(shape) - 1 - axis_at))
    return loudness


def split_up(number_of, total, reach, slope):
    weights = [(1 << 20) // math.isqrt(standing ** slope) + 1 for standing in range(2, number_of + 1)]
    rest, counts = total - reach - (number_of - 1), [1] * (number_of - 1)
    while rest > 0:
        movable = [i for i in range(number_of - 1) if counts[i] < reach]
        whole, left = sum([weights[i] for i in movable]), rest
        for i in movable:
            addition = min(reach - counts[i], max(1, left * weights[i] // whole), rest)
            counts[i] = counts[i] + addition
            rest = rest - addition
    return np.array([reach] + counts)


def ragged_sizes(stream_key, count, total, bound, lean):
    if count == 2:
        one = jax.random.randint(stream_key, (), max(1, total - bound), min(bound, total - 1) + 1)
        return jnp.stack([one, total - one])
    sizes = jnp.asarray(split_up(count, total, bound, lean), jnp.int32)
    pairs = (count - 1) // 2
    giver, receiver = sizes[1:1 + 2 * pairs:2], sizes[2:2 + 2 * pairs:2]
    slack = jnp.minimum(giver - 1, bound - receiver)
    passed = jax.random.randint(jax.random.fold_in(stream_key, 1), (pairs,), 0, 1 << 20) % (slack + 1)
    sizes = sizes.at[1:1 + 2 * pairs:2].set(giver - passed).at[2:2 + 2 * pairs:2].set(receiver + passed)
    return sizes[jax.random.permutation(jax.random.fold_in(stream_key, 2), count)]


def routed_block(stream_key, own, number, rows, count, top, reach, slope):
    order = jax.random.permutation(stream_key, count)
    heavy_load, common = portions_of(count, rows * top, reach, slope, True), portions_of(count, rows * top, reach, slope, False)
    places = jnp.arange(count)

    def named(tallies, rotation):
        used = int((tallies > 0).sum())
        fixed = max(1, used // 4)
        passed = fixed + (places - fixed + rotation * (used - fixed)) % max(1, count - fixed)
        return jnp.zeros((count,), jnp.int32).at[order[jnp.where(places < fixed, places, passed)]].set(jnp.asarray(tallies, jnp.int32))

    tallies = jnp.where(number % 4 == 0, named(heavy_load, number // 4), named(common, number - number // 4 - 1))
    mixed = jax.random.permutation(jax.random.fold_in(own, 3), count)
    source_of, receiver = mixed[0:count // 2 * 2:2], mixed[1:count // 2 * 2:2]
    room = jnp.minimum(tallies[source_of] - 1, reach - tallies[receiver]) // 2
    room = jnp.where((source_of == order[0]) | (receiver == order[0]) | (tallies[receiver] == 0), 0, jnp.maximum(room, 0))
    passed = jax.random.randint(jax.random.fold_in(own, 4), (count // 2,), 0, 1 << 20) % (room + 1)
    tallies = tallies.at[source_of].add(-passed).at[receiver].add(passed)
    members = jnp.searchsorted(jnp.cumsum(tallies), jnp.arange(rows * top), side="right").astype(jnp.int32)
    listing = members.reshape(top, rows).T
    listing = listing[jax.random.permutation(jax.random.fold_in(own, 1), rows)]
    rotation = jax.random.randint(jax.random.fold_in(own, 2), (rows, 1), 0, top)
    return jnp.take_along_axis(listing, (jnp.arange(top)[None, :] + rotation) % top, axis=1)


def portions_of(amount, total, limit, slope, full):
    portions = [(1 << 20) // math.isqrt(grade ** slope) + 1 for grade in range(1, amount + 1)]
    largest = limit if full else min(limit, max(-(-total // amount), total * portions[0] // sum(portions)))
    least = 1 if total - largest >= amount - 1 else 0
    holding, spare = [largest] + [least] * (amount - 1), total - largest - least * (amount - 1)
    while spare > 0:
        free = [i for i in range(1, amount) if holding[i] < largest] or [i for i in range(1, amount) if holding[i] < limit]
        pool, remaining = sum([portions[i] for i in free]), spare
        for i in free:
            more = min(limit - holding[i], max(1, remaining * portions[i] // pool), spare)
            holding[i] = holding[i] + more
            spare = spare - more
    return np.array(holding)


def normal_values(key, shape, width, limit, split=(), kind=jnp.bfloat16):
    result = width * jax.random.normal(key, shape, jnp.float32)
    if split:
        result = result * shard_levels(key, shape, split, -0.22, 0.18)
    return jnp.clip(result, -limit, limit).astype(kind)


def setup_inputs(seed: int = 0) -> dict:
    keys = jax.random.split(jax.random.key(seed), 14)
    resid = normal_values(keys[0], (REQUESTS, D), 0.25, 1.5, ((0, 256),))
    query = draw_query(jax.random.fold_in(keys[13], 71), 0)
    fresh_kv = draw_fresh_kv(jax.random.fold_in(keys[13], 71), 0)
    cache_home = jax.vmap(lambda own: jax.random.permutation(own, BATCH))(jax.random.split(keys[3], N_TIER)).reshape((N_TIER, BATCH)).astype(jnp.int32)
    kv_cache = draw_kv_cache(jax.random.fold_in(keys[13], 71), 0)
    cached_len = ragged_sizes(keys[5], REQUESTS, REQUESTS * CTX // 2, CTX, 2).astype(jnp.int32)
    wo = normal_values(keys[6], (H * HD, D), (H * HD) ** -0.5, 0.0625, ((0, 64),))
    norm_gain = jnp.clip(1.0 + 0.18 * jax.random.normal(keys[7], (D,), jnp.float32), 0.099609375, 1.8984375).astype(jnp.bfloat16)
    w_router = normal_values(keys[8], (D, EXPERTS), D ** -0.5, 0.0625)
    expert_ids_keys = jax.random.split(jax.random.fold_in(keys[9], 1), REQUESTS // BATCH)
    expert_ids_turns = jax.random.permutation(jax.random.fold_in(keys[9], 3), REQUESTS // BATCH)
    expert_ids = jax.vmap(lambda own, number: routed_block(jax.random.fold_in(keys[9], 2), own, number, BATCH, EXPERTS, 2, CAP, 2))(expert_ids_keys, expert_ids_turns).reshape((REQUESTS, 2))
    w_gate = normal_values(keys[10], (EXPERTS, FF, D), D ** -0.5, 0.0625, ((0, 4), (1, 64)))
    w_up = normal_values(keys[11], (EXPERTS, FF, D), D ** -0.5, 0.0625, ((0, 4), (1, 64)))
    w_down = normal_values(keys[12], (EXPERTS, FF, D), FF ** -0.5, 0.0546875, ((0, 4), (1, 64)))
    return dict(resid=resid, query=query, fresh_kv=fresh_kv, cache_home=cache_home, kv_cache=kv_cache, cached_len=cached_len, wo=wo, norm_gain=norm_gain, w_router=w_router, expert_ids=expert_ids, w_gate=w_gate, w_up=w_up, w_down=w_down)


def attend(q_rows, fresh_rows, cache_rows, lengths):
    row_count = q_rows.shape[0]
    per_kv = H // G
    queries = q_rows.reshape(row_count, G, per_kv, HD).astype(jnp.float32)
    cached_keys = cache_rows[:, :, :G * HD].reshape(row_count, CTX, G, HD).astype(jnp.float32)
    cached_values = cache_rows[:, :, G * HD:].reshape(row_count, CTX, G, HD).astype(jnp.float32)
    new_key = fresh_rows[:, :G * HD].reshape(row_count, G, HD).astype(jnp.float32)
    new_value = fresh_rows[:, G * HD:].reshape(row_count, G, HD).astype(jnp.float32)
    score_scale = 1.0 / math.sqrt(HD)
    scores = jnp.einsum('ngqd,npgd->ngqp', queries, cached_keys) * score_scale
    is_live = jnp.arange(CTX, dtype=jnp.int32)[None, None, None, :] < lengths[:, None, None, None]
    scores = jnp.where(is_live, scores, -1e+30)
    own_score = jnp.einsum('ngqd,ngd->ngq', queries, new_key) * score_scale
    row_top = jnp.maximum(lax.optimization_barrier(jnp.max(scores, axis=-1)), own_score)
    weights = jnp.exp(scores - row_top[..., None])
    own_weight = jnp.exp(own_score - row_top)
    denominator = lax.optimization_barrier(jnp.sum(weights, axis=-1)) + own_weight
    weights = lax.optimization_barrier((weights / denominator[..., None]).astype(jnp.bfloat16)).astype(jnp.float32)
    own_weight = lax.optimization_barrier((own_weight / denominator).astype(jnp.bfloat16)).astype(jnp.float32)
    mixture = jnp.einsum('ngqp,npgd->ngqd', weights, cached_values) + own_weight[..., None] * new_value[:, :, None, :]
    return mixture.reshape(row_count, H * HD).astype(jnp.bfloat16)

def gates_of(logits, expert_ids):
    labels = jnp.arange(logits.shape[1], dtype=jnp.int32)
    chosen_mask = (expert_ids[:, :, None] == labels[None, None, :]).astype(jnp.float32)
    chosen = lax.optimization_barrier(jnp.sum(chosen_mask * logits[:, None, :], axis=-1))
    first_gate = 1.0 / (1.0 + jnp.exp(chosen[:, 1] - chosen[:, 0]))
    second_gate = 1.0 / (1.0 + jnp.exp(chosen[:, 0] - chosen[:, 1]))
    return chosen_mask[:, 0, :] * first_gate[:, None] + chosen_mask[:, 1, :] * second_gate[:, None]

def by_width(rows, weight):
    return lax.dot_general(rows, weight, (((1,), (1,)), ((), ())), preferred_element_type=jnp.float32)

def reference(resid, query, fresh_kv, cache_home, kv_cache, cached_len, wo, norm_gain, w_router, expert_ids, w_gate, w_up, w_down):
    row_base = (jnp.arange(N_TIER, dtype=jnp.int32) * BATCH)[:, None]
    slot_of = (cache_home.astype(jnp.int32) + row_base).reshape(-1)
    holder = (jnp.argsort(cache_home, axis=1).astype(jnp.int32) + row_base).reshape(-1)
    by_slot = attend(query[holder], fresh_kv[holder], kv_cache, cached_len)
    attended = by_slot[slot_of]
    hidden = resid.astype(jnp.float32) + jnp.dot(attended, wo, preferred_element_type=jnp.float32)
    spread = lax.rsqrt(lax.optimization_barrier(jnp.mean(hidden * hidden, axis=-1, keepdims=True)) + 1e-05)
    normed = (hidden * spread * norm_gain.astype(jnp.float32)[None, :]).astype(jnp.bfloat16)
    logits = jnp.dot(normed, w_router, preferred_element_type=jnp.float32)
    gate_table = gates_of(logits, expert_ids)
    moe = jnp.zeros(hidden.shape, jnp.float32)
    for expert in range(EXPERTS):
        gate_part = by_width(normed, w_gate[expert])
        up_part = by_width(normed, w_up[expert])
        activation = (jax.nn.silu(gate_part) * up_part).astype(jnp.bfloat16)
        moe = moe + gate_table[:, expert:expert + 1] * jnp.dot(activation, w_down[expert], preferred_element_type=jnp.float32)
    return (hidden + moe).astype(jnp.bfloat16)
```

```python
import functools
import math

import jax
import jax.numpy as jnp
from jax import lax
from jax.experimental import pallas as pl
from jax.experimental.pallas import tpu as pltpu
from jax.sharding import PartitionSpec as P

MESH = pl.DeviceIdType.MESH
F32 = jnp.float32
BF16 = jnp.bfloat16
CZ = 3072
CX = 8192 - CZ
SZ = CZ // 128
SX = CX // 128
TN = 512


def iota(shape, dim):
    return lax.broadcasted_iota(jnp.int32, shape, dim)


def nt(a, b):
    return lax.dot_general(a, b, (((1,), (1,)), ((), ())), preferred_element_type=F32)


def nn(a, b):
    return jnp.dot(a, b, preferred_element_type=F32)


def kernel(
    home_ref, len_ref, ids_ref, query_ref, fresh_ref, resid_ref, gain_ref, router_ref,
    cache_hbm, wo_hbm, gate_hbm, up_hbm, down_hbm,
    out_ref,
    cache, wo, w_in, w_down, local_sem,
    a1s, a1r, a2s, a2r, c1s, c1r, c2s, c2r,
    r1zs, r1zr, r1xs, r1xr, r2zs, r2zr, r2xs, r2xr,
    hid, g1s, g1r, g1f, xa, xb, acc, act,
    f0s, f0r, f1s, f1ra, f1rb, f2sa, f2sb, f2ra, f2rb, f3f, f3s, f3r,
    sa1, sa2, sc1, sc2, sr1z, sr1x, sr2z, sr2x, sg1, sg2, sg3, sg4, sf0, sf1, sf2, sf3,
):
    tier, grp = lax.axis_index("tier"), lax.axis_index("grp")
    y_hi, core = tier // 2, tier % 2
    y_lo, z, x = grp // 32, (grp // 4) % 8, grp % 4
    y = y_hi * 2 + y_lo
    xy = y_lo * 4 + x
    zc = z * 2 + core

    def device(y, z, x, core):
        return ((y // 2) * 2 + core, (y % 2) * 32 + z * 4 + x)

    def send(src, dst, sems, k, to):
        copy = pltpu.make_async_remote_copy(
            src_ref=src, dst_ref=dst, send_sem=sems.at[0, k], recv_sem=sems.at[1, k],
            device_id=to, device_id_type=MESH,
        )
        copy.start()
        return copy

    z_peers = [((z + k) % 8, device(y, (z + k) % 8, x, core)) for k in range(1, 8)]
    xy_peers = []
    for k in range(1, 8):
        px, pl_lo = (x + k) % 4, (y_lo + k // 4) % 2
        xy_peers.append((pl_lo * 4 + px, device(y_hi * 2 + pl_lo, z, px, core)))
    zc_peers = []
    for k in range(1, 16):
        pz, pc = (z + k // 2) % 8, (core + k % 2) % 2
        zc_peers.append((pz * 2 + pc, device(y, pz, x, pc)))
    x_peers = [((x + k) % 4, device(y, z, (x + k) % 4, core)) for k in range(1, 4)]
    y_peers = [((y + k) % 4, device((y + k) % 4, z, x, core)) for k in range(1, 4)]
    sibling = device(y, z, x, 1 - core)
    far = [device(((1 - y_hi) * 2 + (y_lo + k) % 2), z, x, core) for k in range(2)]

    loads = [
        pltpu.make_async_copy(cache_hbm.at[0], cache, local_sem.at[0]),
        pltpu.make_async_copy(wo_hbm, wo, local_sem.at[1]),
        pltpu.make_async_copy(gate_hbm.at[0], w_in.at[0], local_sem.at[2]),
        pltpu.make_async_copy(up_hbm.at[0], w_in.at[1], local_sem.at[3]),
        pltpu.make_async_copy(down_hbm.at[0], w_down, local_sem.at[4]),
    ]
    for load in loads:
        load.start()

    barrier = pltpu.get_barrier_semaphore()
    greeted = [d for _, d in zc_peers] + [d for _, d in xy_peers] + far
    for d in greeted:
        pl.semaphore_signal(barrier, inc=1, device_id=d, device_id_type=MESH)

    slot = home_ref[...]
    place = ((slot >> 2) & 7) * 8 + (slot >> 5) * 4 + (slot & 3)
    to_slot = (iota((64, 64), 0) == place).astype(BF16)
    spread_fresh = (iota((32, 128), 1) == iota((32, 128), 0) + 32 * x).astype(BF16)
    fresh_wide = nn(fresh_ref[...], spread_fresh).astype(BF16)
    by_slot_q = nn(to_slot, query_ref[...])
    by_slot_f = nn(to_slot, fresh_wide)
    for k in range(8):
        a1s[k * 16 : k * 16 + 8] = by_slot_q[k * 8 : k * 8 + 8]
        a1s[k * 16 + 8 : k * 16 + 16] = by_slot_f[k * 8 : k * 8 + 8]

    pl.semaphore_wait(barrier, len(greeted))

    def rows(ref, i, n):
        return ref.at[pl.ds(pl.multiple_of(i * n, n), n)]

    pending = []
    copies = [
        send(rows(a1s, p, 16), rows(a1r, z, 16), sa1, k, d) for k, (p, d) in enumerate(z_peers)
    ]
    rows(a1r, z, 16)[...] = rows(a1s, z, 16)[...]
    for c in copies:
        c.wait_recv()
    pending += copies
    for k in range(8):
        for half in range(2):
            a2s[k * 16 + half * 8 : k * 16 + half * 8 + 8] = a1r[pl.ds(half * 8 + k, 8, stride=16), :]
    copies = [
        send(rows(a2s, p, 16), rows(a2r, xy, 16), sa2, k, d) for k, (p, d) in enumerate(xy_peers)
    ]
    rows(a2r, xy, 16)[...] = rows(a2s, xy, 16)[...]
    for c in copies:
        c.wait_recv()
    pending += copies

    head = iota((64, 128), 0)
    group = (head >> 5) * 4 + ((head & 7) >> 1)
    got = a2r[...].reshape(8, 16, 128)
    queries = got[:, :8].reshape(64, 128)
    news = got[:, 8:]
    new_key = (news[0] + news[1] + news[2] + news[3]).astype(BF16)
    new_value = (news[4] + news[5] + news[6] + news[7]).astype(BF16)
    of_group = (iota((64, 8), 1) == (iota((64, 8), 0) >> 5) * 4 + ((iota((64, 8), 0) & 7) >> 1)).astype(BF16)
    own_key = nn(of_group, new_key)
    own_value = nn(of_group, new_value)
    loads[0].wait()
    wide = jnp.concatenate(
        [jnp.where(group == j, queries, 0.0).astype(BF16) for j in range(8)], axis=1
    )
    scale = 1.0 / math.sqrt(128)
    scores = nt(wide, cache[:, :1024]) * scale
    scores = jnp.where(iota((64, 128), 1) < len_ref[0], scores, -1e30)
    own_score = jnp.sum(queries * own_key, axis=1, keepdims=True) * scale
    top = jnp.maximum(jnp.max(scores, axis=1, keepdims=True), own_score)
    weights = jnp.exp(scores - top)
    own_weight = jnp.exp(own_score - top)
    denominator = jnp.sum(weights, axis=1, keepdims=True) + own_weight
    weights = (weights / denominator).astype(BF16)
    own_weight = (own_weight / denominator).astype(BF16).astype(F32)
    mixed = nn(weights, cache[:, 1024:])
    outcome = own_weight * own_value
    for j in range(8):
        outcome = outcome + jnp.where(group == j, mixed[:, j * 128 : (j + 1) * 128], 0.0)
    c1s[...] = outcome.astype(BF16).astype(F32)

    copies = [
        send(rows(c1s, p, 8), rows(c1r, xy, 8), sc1, k, d) for k, (p, d) in enumerate(xy_peers)
    ]
    rows(c1r, xy, 8)[...] = rows(c1s, xy, 8)[...]
    for c in copies:
        c.wait_recv()
    pending += copies
    for k in range(8):
        c2s[k * 8 : k * 8 + 8] = c1r[pl.ds(k, 8, stride=8), :]
    copies = [
        send(rows(c2s, p, 8), rows(c2r, z, 8), sc2, k, d) for k, (p, d) in enumerate(z_peers)
    ]
    rows(c2r, z, 8)[...] = rows(c2s, z, 8)[...]
    for c in copies:
        c.wait_recv()
    pending += copies

    own = iota((64, 64), 1)
    own_z, own_xy = (own >> 2) & 7, (own >> 5) * 4 + (own & 3)
    by_head = c2r[...].astype(BF16)
    order_z = (iota((64, 64), 0) == own_z * 8 + own_xy).astype(BF16)
    order_x = (iota((64, 64), 0) == own_xy * 8 + own_z).astype(BF16)
    att_z = nn(nt(order_z, to_slot).astype(BF16), by_head).astype(BF16)
    att_x = nn(nt(order_x, to_slot).astype(BF16), by_head).astype(BF16)
    loads[1].wait()

    def project(att, ref, base, width):
        def tile(t, _):
            at = pl.multiple_of(t * TN, TN)
            lo = nn(att, wo[:, pl.ds(base + at, TN)]).reshape(8, 8, TN)
            hi = nn(att, wo[:, pl.ds(base + width + at, TN)]).reshape(8, 8, TN)
            ref[:, :, pl.ds(at, TN)] = jnp.concatenate([lo, hi], axis=1).astype(BF16)
            return 0

        lax.fori_loop(0, width // TN, tile, 0)

    project(att_z, r1zs, 0, CZ // 2)
    copies_z = [send(r1zs.at[p], r1zr.at[k], sr1z, k, d) for k, (p, d) in enumerate(z_peers)]
    project(att_x, r1xs, CZ, CX // 2)
    copies_x = [send(r1xs.at[p], r1xr.at[k], sr1x, k, d) for k, (p, d) in enumerate(xy_peers)]
    pending += copies_z + copies_x

    def fold(sent, mine, received, n, slabs, stride):
        def tile(j, _):
            at = pl.multiple_of(j * 128, 128)
            total = sent[mine, :, pl.ds(at, 128)].astype(F32)
            for k in range(n):
                total = total + received[k, :, pl.ds(at, 128)].astype(F32)
            slabs[pl.ds(j, 8, stride=stride), :] = total[:8]
            slabs[pl.ds(j + stride // 2, 8, stride=stride), :] = total[8:]
            return 0

        lax.fori_loop(0, stride // 2, tile, 0)

    for c in copies_z:
        c.wait_recv()
    fold(r1zs, z, r1zr, 7, r2zs, SZ)
    copies_z = [
        send(rows(r2zs, p, SZ), r2zr.at[k], sr2z, k, d) for k, (p, d) in enumerate(xy_peers)
    ]
    for c in copies_x:
        c.wait_recv()
    fold(r1xs, xy, r1xr, 7, r2xs, SX)
    copies_x = [
        send(rows(r2xs, p, SX), r2xr.at[k], sr2x, k, d) for k, (p, d) in enumerate(z_peers)
    ]
    for c in copies_z + copies_x:
        c.wait_recv()
    pending += copies_z + copies_x
    part_z, part_x = rows(r2zs, xy, SZ)[...], rows(r2xs, z, SX)[...]
    for k in range(7):
        part_z = part_z + r2zr[k]
        part_x = part_x + r2xr[k]
    hidden = resid_ref[...].astype(F32) + jnp.concatenate([part_z, part_x], axis=0)
    hid[...] = hidden

    mean = jnp.sum(hidden * hidden, keepdims=True) * (1.0 / 8192)
    normed = (hidden * lax.rsqrt(mean + 1e-05) * gain_ref[...].astype(F32)).astype(BF16)
    normed_wide = normed.astype(F32)
    logits = [
        jnp.sum(normed_wide * router_ref[e].astype(F32), keepdims=True) for e in range(4)
    ]
    first, second = ids_ref[0, 0], ids_ref[0, 1]
    zero = jnp.zeros((1, 1), F32)
    logit_a, logit_b = zero, zero
    for e in range(4):
        logit_a = logit_a + jnp.where(first == e, logits[e], zero)
        logit_b = logit_b + jnp.where(second == e, logits[e], zero)
    gate_a = 1.0 / (1.0 + jnp.exp(logit_b - logit_a))
    gate_b = 1.0 / (1.0 + jnp.exp(logit_a - logit_b))
    lane = iota((16, 128), 1)
    gate_row = jnp.where((lane & 3) == first, gate_a, 0.0) + jnp.where((lane & 3) == second, gate_b, 0.0)
    gate_high = gate_row.astype(BF16).astype(F32)
    gate_pair = jnp.where(lane < 4, gate_high, jnp.where(lane < 8, gate_row - gate_high, 0.0)).astype(BF16)
    for c in range(2):
        g1s[c * 48 : c * 48 + 32] = normed[c * 32 : c * 32 + 32]
        g1s[c * 48 + 32 : c * 48 + 48] = gate_pair

    copies = []
    for k, (p, d) in enumerate(zc_peers):
        copies.append(send(rows(g1s, p % 2, 48), rows(g1r, zc, 48), sg1, k, d))
    rows(g1r, zc, 48)[...] = rows(g1s, core, 48)[...]
    for c in copies:
        c.wait_recv()
    pending += copies
    g1f[...] = g1r[...].astype(F32)
    for j in range(16):
        xa[core, y, x, :, j * 128 : j * 128 + 128] = g1f[pl.ds(j, 16, stride=48), :].astype(BF16)
    for j in range(17):
        xb[core, y, x, :, j * 128 : j * 128 + 128] = g1f[pl.ds(16 + j, 16, stride=48), :].astype(BF16)

    first_a = [send(xa.at[core, y, x], xa.at[core, y, x], sg2, k, d) for k, (p, d) in enumerate(y_peers)]
    first_b = [send(xb.at[core, y, x], xb.at[core, y, x], sg2, 3 + k, d) for k, (p, d) in enumerate(x_peers)]
    for c in first_a + first_b:
        c.wait_recv()
    then_a = [send(xa.at[core, :, x], xa.at[core, :, x], sg3, k, d) for k, (p, d) in enumerate(x_peers)]
    then_b = [send(xb.at[core, y], xb.at[core, y], sg3, 3 + k, d) for k, (p, d) in enumerate(y_peers)]
    across = [
        send(xa.at[core, :, x], xa.at[core, :, x], sg4, 0, sibling),
        send(xb.at[core, y], xb.at[core, y], sg4, 4, sibling),
    ]
    for k in range(3):
        from_x, from_y = (x + 3 - k) % 4, (y + 3 - k) % 4
        then_a[k].wait_recv()
        across.append(send(xa.at[core, :, from_x], xa.at[core, :, from_x], sg4, 1 + k, sibling))
        then_b[k].wait_recv()
        across.append(send(xb.at[core, from_y], xb.at[core, from_y], sg4, 5 + k, sibling))
    pending += first_a + first_b + then_a + then_b + across

    for load in loads[2:]:
        load.wait()
    acc[...] = jnp.zeros_like(acc)

    def into(half):
        def tile(t, _):
            at = pl.multiple_of(t * TN, TN)
            for part, ref in ((0, xa), (1, xb)):
                rows_in = ref[half, :, :, :, pl.ds(at, TN)].reshape(256, TN)
                column = pl.ds(pl.multiple_of(half * 4096 + part * 2048 + at, TN), TN)
                acc[0] += nt(rows_in, w_in[0, :, column])
                acc[1] += nt(rows_in, w_in[1, :, column])
            return 0

        lax.fori_loop(0, 2048 // TN, tile, 0)

    into(core)
    for c in across:
        c.wait_recv()
    into(1 - core)
    gate_part = acc[0]
    act[...] = (gate_part / (1.0 + jnp.exp(-gate_part)) * acc[1]).astype(BF16)
    pairs = xb[core, :, :, :, 2048:].reshape(256, 128).astype(F32)
    mine = (iota((256, 128), 1) & 3) == tier
    gate = jnp.sum(jnp.where(mine, pairs, 0.0), axis=1, keepdims=True)

    def down(column):
        return nn(act[...], w_down[:, column]) * gate

    over = []
    for part in range(2):
        def tile(t, _, part=part):
            at = pl.multiple_of(t * TN, TN)
            column = pl.ds(pl.multiple_of((1 - core) * 4096 + part * 2048 + at, TN), TN)
            f0s[part, :, :, :, pl.ds(at, TN)] = down(column).astype(BF16).reshape(4, 4, 16, TN)
            return 0

        lax.fori_loop(0, 2048 // TN, tile, 0)
        over.append(send(f0s.at[part], f0r.at[part], sf0, part, sibling))
    pending += over

    then = []
    for part in range(2):
        over[part].wait_recv()

        def tile(t, _, part=part):
            at = pl.multiple_of(t * TN, TN)
            column = pl.ds(pl.multiple_of(core * 4096 + part * 2048 + at, TN), TN)
            both = down(column) + f0r[part, :, :, :, pl.ds(at, TN)].reshape(256, TN).astype(F32)
            f1s[part, :, :, :, pl.ds(at, TN)] = both.astype(BF16).reshape(4, 4, 16, TN)
            return 0

        lax.fori_loop(0, 2048 // TN, tile, 0)
        if part == 0:
            then.append([send(f1s.at[0, :, p], f1ra.at[k], sf1, k, d) for k, (p, d) in enumerate(x_peers)])
        else:
            then.append([send(f1s.at[1, p], f1rb.at[k], sf1, 3 + k, d) for k, (p, d) in enumerate(y_peers)])
    pending += then[0] + then[1]

    last = []
    for part in range(2):
        for c in then[part]:
            c.wait_recv()

        def tile(t, _, part=part):
            at = pl.ds(pl.multiple_of(t * TN, TN), TN)
            if part == 0:
                total = f1s[0, :, x, :, at].astype(F32)
                for k in range(3):
                    total = total + f1ra[k, :, :, at].astype(F32)
                f2sa[:, :, at] = total.astype(BF16)
            else:
                total = f1s[1, y, :, :, at].astype(F32)
                for k in range(3):
                    total = total + f1rb[k, :, :, at].astype(F32)
                f2sb[:, :, at] = total.astype(BF16)
            return 0

        lax.fori_loop(0, 2048 // TN, tile, 0)
        if part == 0:
            last.append([send(f2sa.at[p], f2ra.at[k], sf2, k, d) for k, (p, d) in enumerate(y_peers)])
        else:
            last.append([send(f2sb.at[p], f2rb.at[k], sf2, 3 + k, d) for k, (p, d) in enumerate(x_peers)])
    pending += last[0] + last[1]
    for c in last[0] + last[1]:
        c.wait_recv()
    for j in range(16):
        at = slice(j * 128, j * 128 + 128)
        total_a, total_b = f2sa[y, :, at].astype(F32), f2sb[x, :, at].astype(F32)
        for k in range(3):
            total_a = total_a + f2ra[k, :, at].astype(F32)
            total_b = total_b + f2rb[k, :, at].astype(F32)
        f3f[pl.ds(j, 16, stride=32), :] = total_a
        f3f[pl.ds(16 + j, 16, stride=32), :] = total_b
    f3s[...] = f3f[...].astype(BF16)
    copies = [send(rows(f3s, p, 32), f3r.at[zc], sf3, k, d) for k, (p, d) in enumerate(zc_peers)]
    f3r[zc] = rows(f3s, zc, 32)[...]
    for c in copies:
        c.wait_recv()
    pending += copies
    low, high = f3r[0].astype(F32), f3r[1].astype(F32)
    for k in range(1, 8):
        low = low + f3r[2 * k].astype(F32)
        high = high + f3r[2 * k + 1].astype(F32)
    out_ref[...] = (hid[...] + jnp.concatenate([low, high], axis=0)).astype(BF16)
    for c in pending:
        c.wait_send()


def on_device(
    resid, query, fresh_kv, cache_home, kv_cache, cached_len, wo, norm_gain, w_router,
    expert_ids, w_gate, w_up, w_down,
):
    vmem, smem, hbm = (
        pl.BlockSpec(memory_space=pltpu.VMEM),
        pl.BlockSpec(memory_space=pltpu.SMEM),
        pl.BlockSpec(memory_space=pl.ANY),
    )
    v = pltpu.VMEM
    sem = lambda n: pltpu.SemaphoreType.DMA((2, n))
    out = pl.pallas_call(
        kernel,
        out_shape=jax.ShapeDtypeStruct((64, 128), BF16),
        in_specs=[vmem, smem, smem, vmem, vmem, vmem, vmem, vmem, hbm, hbm, hbm, hbm, hbm],
        out_specs=vmem,
        scratch_shapes=[
            v((128, 2048), BF16), v((128, 8192), BF16), v((2, 192, 8192), BF16), v((192, 8192), BF16),
            pltpu.SemaphoreType.DMA((5,)),
            v((128, 128), F32), v((128, 128), F32), v((128, 128), F32), v((128, 128), F32),
            v((64, 128), F32), v((64, 128), F32), v((64, 128), F32), v((64, 128), F32),
            v((8, 16, CZ // 2), BF16), v((7, 16, CZ // 2), BF16),
            v((8, 16, CX // 2), BF16), v((7, 16, CX // 2), BF16),
            v((8 * SZ, 128), F32), v((7, SZ, 128), F32), v((8 * SX, 128), F32), v((7, SX, 128), F32),
            v((64, 128), F32), v((96, 128), BF16), v((768, 128), BF16), v((768, 128), F32),
            v((2, 4, 4, 16, 2048), BF16), v((2, 4, 4, 16, 2176), BF16),
            v((2, 256, 192), F32), v((256, 192), BF16),
            v((2, 4, 4, 16, 2048), BF16), v((2, 4, 4, 16, 2048), BF16), v((2, 4, 4, 16, 2048), BF16),
            v((3, 4, 16, 2048), BF16), v((3, 4, 16, 2048), BF16),
            v((4, 16, 2048), BF16), v((4, 16, 2048), BF16), v((3, 16, 2048), BF16), v((3, 16, 2048), BF16),
            v((512, 128), F32), v((512, 128), BF16), v((16, 32, 128), BF16),
            sem(7), sem(7), sem(7), sem(7), sem(7), sem(7), sem(7), sem(7),
            sem(15), sem(6), sem(6), sem(8), sem(2), sem(6), sem(6), sem(15),
        ],
        compiler_params=pltpu.CompilerParams(
            collective_id=0, has_side_effects=True, vmem_limit_bytes=60 * 2**20
        ),
    )(
        cache_home, cached_len, expert_ids, query, fresh_kv, resid.reshape(64, 128),
        norm_gain.reshape(64, 128), jnp.transpose(w_router).reshape(4, 64, 128),
        kv_cache, wo, w_gate, w_up, w_down,
    )
    return out.reshape(1, 8192)


def solution(mesh):
    return jax.shard_map(
        on_device,
        mesh=mesh,
        in_specs=(
            P(("tier", "grp"), None),
            P("tier", "grp"),
            P("tier", "grp"),
            P("tier", None),
            P(("tier", "grp"), None, None),
            P(("tier", "grp")),
            P("grp", None),
            P(),
            P(),
            P(("tier", "grp"), None),
            P("tier", "grp", None),
            P("tier", "grp", None),
            P("tier", "grp", None),
        ),
        out_specs=P(("tier", "grp"), None),
        check_vma=False,
    )
```

```python
import functools
import math

import jax
import jax.numpy as jnp
from jax import lax
from jax.experimental import pallas as pl
from jax.experimental.pallas import tpu as pltpu
from jax.sharding import PartitionSpec as P

MESH = pl.DeviceIdType.MESH
F32 = jnp.float32
BF16 = jnp.bfloat16
CZ = 3072
CX = 8192 - CZ
SZ = CZ // 128
SX = CX // 128
PZ, PX = -(-SZ // 16) * 16, -(-SX // 16) * 16
TN = 512


def iota(shape, dim):
    return lax.broadcasted_iota(jnp.int32, shape, dim)


def nt(a, b):
    return lax.dot_general(a, b, (((1,), (1,)), ((), ())), preferred_element_type=F32)


def nn(a, b):
    return jnp.dot(a, b, preferred_element_type=F32)


def kernel(
    home_ref, len_ref, ids_ref, query_ref, fresh_ref, resid_ref, gain_ref, router_ref,
    cache_hbm, wo_hbm, gate_hbm, up_hbm, down_hbm,
    out_ref,
    cache, wo, w_in, w_down, local_sem,
    a1s, a1r, a2s, a2r, c1s, c1r, c2s, c2r,
    r1zs, r1zr, r1xs, r1xr, r2zs, r2zr, r2xs, r2xr,
    r2fz, r2fx, hid, router,
    g1s, g1r, g1f, gates, gate_in, gate_all, xa, xb, acc, act,
    f0s, f0r, f1s, fo, fd, fcs, fcr, f2s, f2r, f3f, f3s, f3r,
    sa1, sa2, sc1, sc2, sr1z, sr1x, sr2z, sr2x, sg1, sgate, sg2, sg3, sg4, sf0, sf1, sf2, sf3,
):
    tier, grp = lax.axis_index("tier"), lax.axis_index("grp")
    y_hi, core = tier // 2, tier % 2
    y_lo, z, x = grp // 32, (grp // 4) % 8, grp % 4
    y = y_hi * 2 + y_lo
    xy = y_lo * 4 + x
    zc = z * 2 + core

    def device(y, z, x, core):
        return ((y // 2) * 2 + core, (y % 2) * 32 + z * 4 + x)

    def send(src, dst, sems, k, to):
        copy = pltpu.make_async_remote_copy(
            src_ref=src, dst_ref=dst, send_sem=sems.at[0, k], recv_sem=sems.at[1, k],
            device_id=to, device_id_type=MESH,
        )
        copy.start()
        return copy

    z_peers = [((z + k) % 8, device(y, (z + k) % 8, x, core)) for k in range(1, 8)]
    xy_peers = []
    for k in range(1, 8):
        px, pl_lo = (x + k) % 4, (y_lo + k // 4) % 2
        xy_peers.append((pl_lo * 4 + px, device(y_hi * 2 + pl_lo, z, px, core)))
    zc_peers = []
    for k in range(1, 16):
        pz, pc = (z + k // 2) % 8, (core + k % 2) % 2
        zc_peers.append((pz * 2 + pc, device(y, pz, x, pc)))
    x_peers = [((x + k) % 4, device(y, z, (x + k) % 4, core)) for k in range(1, 4)]
    y_peers = [((y + k) % 4, device((y + k) % 4, z, x, core)) for k in range(1, 4)]
    sibling = device(y, z, x, 1 - core)
    far = [device(((1 - y_hi) * 2 + (y_lo + k) % 2), z, x, core) for k in range(2)]

    loads = [
        pltpu.make_async_copy(cache_hbm.at[0], cache, local_sem.at[0]),
        pltpu.make_async_copy(wo_hbm, wo, local_sem.at[1]),
        pltpu.make_async_copy(gate_hbm.at[0], w_in.at[0], local_sem.at[2]),
        pltpu.make_async_copy(up_hbm.at[0], w_in.at[1], local_sem.at[3]),
        pltpu.make_async_copy(down_hbm.at[0], w_down, local_sem.at[4]),
    ]
    for load in loads:
        load.start()

    barrier = pltpu.get_barrier_semaphore()
    greeted = [d for _, d in zc_peers] + [d for _, d in xy_peers] + far
    for d in greeted:
        pl.semaphore_signal(barrier, inc=1, device_id=d, device_id_type=MESH)

    slot = home_ref[...]
    place = ((slot >> 2) & 7) * 8 + (slot >> 5) * 4 + (slot & 3)
    to_slot = (iota((64, 64), 0) == place).astype(BF16)
    spread_fresh = (iota((32, 128), 1) == iota((32, 128), 0) + 32 * x).astype(BF16)
    by_slot_q = nn(to_slot, query_ref[...])
    by_slot_f = nn(nt(to_slot, fresh_ref[...]).astype(BF16), spread_fresh)
    for k in range(8):
        a1s[k * 16 : k * 16 + 8] = by_slot_q[k * 8 : k * 8 + 8]
        a1s[k * 16 + 8 : k * 16 + 16] = by_slot_f[k * 8 : k * 8 + 8]

    resid_row, router_rows = resid_ref[...].astype(F32), router_ref[...].astype(F32)
    for j in range(64):
        hid[j : j + 1] = resid_row[:, j * 128 : j * 128 + 128]
        router[pl.ds(j, 4, stride=64), :] = router_rows[:, j * 128 : j * 128 + 128]
    r2fz[...] = jnp.zeros_like(r2fz)
    r2fx[...] = jnp.zeros_like(r2fx)

    pl.semaphore_wait(barrier, len(greeted))

    def rows(ref, i, n):
        return ref.at[pl.ds(pl.multiple_of(i * n, n), n)]

    pending = []
    copies = [
        send(rows(a1s, p, 16), rows(a1r, z, 16), sa1, k, d) for k, (p, d) in enumerate(z_peers)
    ]
    rows(a1r, z, 16)[...] = rows(a1s, z, 16)[...]
    for c in copies:
        c.wait_recv()
    pending += copies
    for k in range(8):
        for half in range(2):
            a2s[k * 16 + half * 8 : k * 16 + half * 8 + 8] = a1r[pl.ds(half * 8 + k, 8, stride=16), :]
    copies = [
        send(rows(a2s, p, 16), rows(a2r, xy, 16), sa2, k, d) for k, (p, d) in enumerate(xy_peers)
    ]
    rows(a2r, xy, 16)[...] = rows(a2s, xy, 16)[...]
    for c in copies:
        c.wait_recv()
    pending += copies

    head = iota((64, 128), 0)
    group = (head >> 5) * 4 + ((head & 7) >> 1)
    got = a2r[...].reshape(8, 16, 128)
    queries = got[:, :8].reshape(64, 128)
    news = got[:, 8:]
    new_key = (news[0] + news[1] + news[2] + news[3]).astype(BF16)
    new_value = (news[4] + news[5] + news[6] + news[7]).astype(BF16)
    of_group = (iota((64, 8), 1) == (iota((64, 8), 0) >> 5) * 4 + ((iota((64, 8), 0) & 7) >> 1)).astype(BF16)
    own_key = nn(of_group, new_key)
    own_value = nn(of_group, new_value)
    loads[0].wait()
    wide = jnp.concatenate(
        [jnp.where(group == j, queries, 0.0).astype(BF16) for j in range(8)], axis=1
    )
    scale = 1.0 / math.sqrt(128)
    scores = nt(wide, cache[:, :1024]) * scale
    scores = jnp.where(iota((64, 128), 1) < len_ref[0], scores, -1e30)
    own_score = jnp.sum(queries * own_key, axis=1, keepdims=True) * scale
    top = jnp.maximum(jnp.max(scores, axis=1, keepdims=True), own_score)
    weights = jnp.exp(scores - top)
    own_weight = jnp.exp(own_score - top)
    denominator = jnp.sum(weights, axis=1, keepdims=True) + own_weight
    weights = (weights / denominator).astype(BF16)
    own_weight = (own_weight / denominator).astype(BF16).astype(F32)
    mixed = nn(weights, cache[:, 1024:])
    outcome = own_weight * own_value
    for j in range(8):
        outcome = outcome + jnp.where(group == j, mixed[:, j * 128 : (j + 1) * 128], 0.0)
    c1s[...] = outcome.astype(BF16).astype(F32)

    copies = [
        send(rows(c1s, p, 8), rows(c1r, xy, 8), sc1, k, d) for k, (p, d) in enumerate(xy_peers)
    ]
    rows(c1r, xy, 8)[...] = rows(c1s, xy, 8)[...]
    for c in copies:
        c.wait_recv()
    pending += copies
    for k in range(8):
        c2s[k * 8 : k * 8 + 8] = c1r[pl.ds(k, 8, stride=8), :]
    copies = [
        send(rows(c2s, p, 8), rows(c2r, z, 8), sc2, k, d) for k, (p, d) in enumerate(z_peers)
    ]
    rows(c2r, z, 8)[...] = rows(c2s, z, 8)[...]
    for c in copies:
        c.wait_recv()
    pending += copies

    own = iota((64, 64), 1)
    own_z, own_xy = (own >> 2) & 7, (own >> 5) * 4 + (own & 3)
    by_head = c2r[...].astype(BF16)
    order_z = (iota((64, 64), 0) == own_z * 8 + own_xy).astype(BF16)
    order_x = (iota((64, 64), 0) == own_xy * 8 + own_z).astype(BF16)
    att_z = nn(nt(order_z, to_slot).astype(BF16), by_head).astype(BF16)
    att_x = nn(nt(order_x, to_slot).astype(BF16), by_head).astype(BF16)
    loads[1].wait()

    def project(att, ref, base, width):
        def tile(t, _):
            at = pl.multiple_of(t * TN, TN)
            lo = nn(att, wo[:, pl.ds(base + at, TN)]).reshape(8, 8, TN)
            hi = nn(att, wo[:, pl.ds(base + width + at, TN)]).reshape(8, 8, TN)
            ref[:, :, pl.ds(at, TN)] = jnp.concatenate([lo, hi], axis=1).astype(BF16)
            return 0

        lax.fori_loop(0, width // TN, tile, 0)

    project(att_z, r1zs, 0, CZ // 2)
    copies_z = [send(r1zs.at[p], r1zr.at[k], sr1z, k, d) for k, (p, d) in enumerate(z_peers)]
    project(att_x, r1xs, CZ, CX // 2)
    copies_x = [send(r1xs.at[p], r1xr.at[k], sr1x, k, d) for k, (p, d) in enumerate(xy_peers)]
    pending += copies_z + copies_x

    def fold(sent, mine, received, n, slabs, used, stride):
        def tile(j, _):
            at = pl.multiple_of(j * 128, 128)
            total = sent[mine, :, pl.ds(at, 128)].astype(F32)
            for k in range(n):
                total = total + received[k, :, pl.ds(at, 128)].astype(F32)
            slabs[pl.ds(j, 8, stride=stride), :] = total[:8]
            slabs[pl.ds(j + used // 2, 8, stride=stride), :] = total[8:]
            return 0

        lax.fori_loop(0, used // 2, tile, 0)

    for c in copies_z:
        c.wait_recv()
    fold(r1zs, z, r1zr, 7, r2fz, SZ, PZ)
    r2zs[...] = r2fz[...].astype(BF16)
    copies_z = [
        send(rows(r2zs, p, PZ), r2zr.at[k], sr2z, k, d) for k, (p, d) in enumerate(xy_peers)
    ]
    for c in copies_x:
        c.wait_recv()
    fold(r1xs, xy, r1xr, 7, r2fx, SX, PX)
    r2xs[...] = r2fx[...].astype(BF16)
    copies_x = [
        send(rows(r2xs, p, PX), r2xr.at[k], sr2x, k, d) for k, (p, d) in enumerate(z_peers)
    ]
    for c in copies_z + copies_x:
        c.wait_recv()
    pending += copies_z + copies_x
    part_z, part_x = rows(r2fz, xy, PZ)[...], rows(r2fx, z, PX)[...]
    for k in range(7):
        part_z = part_z + r2zr[k].astype(F32)
        part_x = part_x + r2xr[k].astype(F32)
    hidden = hid[...] + jnp.concatenate([part_z[:SZ], part_x[:SX]], axis=0)
    hid[...] = hidden

    mean = jnp.sum(hidden * hidden, keepdims=True) * (1.0 / 8192)
    normed = (hidden * lax.rsqrt(mean + 1e-05) * gain_ref[...].astype(F32)).astype(BF16)
    normed_wide = normed.astype(F32)
    logits = [
        jnp.sum(normed_wide * router[e * 64 : e * 64 + 64], keepdims=True) for e in range(4)
    ]
    first, second = ids_ref[0, 0], ids_ref[0, 1]
    zero = jnp.zeros((1, 1), F32)
    logit_a, logit_b = zero, zero
    for e in range(4):
        logit_a = logit_a + jnp.where(first == e, logits[e], zero)
        logit_b = logit_b + jnp.where(second == e, logits[e], zero)
    gate_a = 1.0 / (1.0 + jnp.exp(logit_b - logit_a))
    gate_b = 1.0 / (1.0 + jnp.exp(logit_a - logit_b))
    lane = iota((8, 128), 1)
    gates[...] = jnp.where(lane == first, gate_a, 0.0) + jnp.where(lane == second, gate_b, 0.0)
    g1s[...] = normed

    copies = [
        send(rows(g1s, p % 2, 32), rows(g1r, zc, 32), sg1, k, d) for k, (p, d) in enumerate(zc_peers)
    ]
    gate_copies = [
        send(gates.at[pl.ds(0, 1)], gate_in.at[zc, pl.ds(0, 1)], sgate, k, d)
        for k, (p, d) in enumerate(zc_peers)
    ]
    rows(g1r, zc, 32)[...] = rows(g1s, core, 32)[...]
    gate_in[zc] = gates[...]
    for c in copies:
        c.wait_recv()
    pending += copies + gate_copies
    g1f[...] = g1r[...].astype(F32)
    for j in range(16):
        xa[core, y, x, :, j * 128 : j * 128 + 128] = g1f[pl.ds(j, 16, stride=32), :].astype(BF16)
    for j in range(16):
        xb[core, y, x, :, j * 128 : j * 128 + 128] = g1f[pl.ds(16 + j, 16, stride=32), :].astype(BF16)

    def block(part, j, i):
        if part == 0:
            return xa.at[core, (y + 4 - j) % 4, (x + 4 - i) % 4]
        return xb.at[core, (y + 4 - i) % 4, (x + 4 - j) % 4]

    def line(part, i):
        if part == 0:
            return xa.at[core, :, (x + 4 - i) % 4]
        return xb.at[core, (y + 4 - i) % 4]

    first_axis = [[d for _, d in y_peers], [d for _, d in x_peers]]
    second_axis = [[d for _, d in x_peers], [d for _, d in y_peers]]
    across = []
    middle = [[], []]
    onward = [{}, {}]

    def pass_on(part, j):
        for to, k in ((0, 0), (2, 4)):
            ref = block(part, j, 0)
            onward[part][k + j] = send(ref, ref, sg3, part * 12 + k + j, second_axis[part][to])
        ref = block(part, j, 0)
        across.append(send(ref, ref, sg4, part * 7 + j, sibling))

    def relay(part, j):
        if j % 2 == 0:
            onward[part][j].wait_recv()
            ref, to = block(part, j, 1), second_axis[part][0]
        else:
            onward[part][4 + j].wait_recv()
            ref, to = block(part, j, 3), second_axis[part][2]
        onward[part][8 + j] = send(ref, ref, sg3, part * 12 + 8 + j, to)

    for part in range(2):
        ref = block(part, 0, 0)
        for k in range(3):
            middle[part].append(send(ref, ref, sg2, part * 3 + k, first_axis[part][k]))
        pass_on(part, 0)
    for j in (1, 3):
        for part in range(2):
            middle[part][j - 1].wait_recv()
            pass_on(part, j)
    for part in range(2):
        relay(part, 0)
    for part in range(2):
        middle[part][1].wait_recv()
        pass_on(part, 2)
    for j in (1, 3, 2):
        for part in range(2):
            relay(part, j)
    for c in gate_copies:
        c.wait_recv()
    for i in range(16):
        gate_all[y, x, i : i + 1] = gate_in[i, 0:1]
    ref = gate_all.at[y, x]
    gate_middle = [send(ref, ref, sgate, 15 + k, d) for k, d in enumerate(first_axis[0])]
    for part in range(2):
        for j in (1, 3):
            onward[part][j].wait_recv()
        across.append(send(line(part, 1), line(part, 1), sg4, part * 7 + 4, sibling))
        for j in (0, 2):
            onward[part][4 + j].wait_recv()
        across.append(send(line(part, 3), line(part, 3), sg4, part * 7 + 5, sibling))
    for c in gate_middle:
        c.wait_recv()
    ref = gate_all.at[:, x]
    gate_onward = [send(ref, ref, sgate, 18 + k, d) for k, d in enumerate(second_axis[0])]
    for part in range(2):
        for j in range(4):
            onward[part][8 + j].wait_recv()
        across.append(send(line(part, 2), line(part, 2), sg4, part * 7 + 6, sibling))
    pending += across + gate_middle + gate_onward
    for part in range(2):
        pending += middle[part] + list(onward[part].values())

    for load in loads[2:]:
        load.wait()
    acc[...] = jnp.zeros_like(acc)

    def into(half):
        def tile(t, _):
            at = pl.multiple_of(t * TN, TN)
            for part, ref in ((0, xa), (1, xb)):
                rows_in = ref[half, :, :, :, pl.ds(at, TN)].reshape(256, TN)
                column = pl.ds(pl.multiple_of(half * 4096 + part * 2048 + at, TN), TN)
                acc[0] += nt(rows_in, w_in[0, :, column])
                acc[1] += nt(rows_in, w_in[1, :, column])
            return 0

        lax.fori_loop(0, 2048 // TN, tile, 0)

    into(core)
    for c in across:
        c.wait_recv()
    into(1 - core)
    gate_part = acc[0]
    act[...] = (gate_part / (1.0 + jnp.exp(-gate_part)) * acc[1]).astype(BF16)
    for c in gate_onward:
        c.wait_recv()
    mine = iota((256, 128), 1) == tier
    gate = jnp.sum(jnp.where(mine, gate_all[...].reshape(256, 128), 0.0), axis=1, keepdims=True)

    def down(half, part, t):
        column = pl.ds(pl.multiple_of(half * 4096 + part * 2048 + t * TN, TN), TN)
        return nn(act[...], w_down[:, column]) * gate

    chunks = range(4)

    def cut(t):
        return slice(t * TN, t * TN + TN)

    over = {}
    for t in chunks:
        for part in range(2):
            f0s[part, :, :, :, cut(t)] = down(1 - core, part, t).astype(BF16).reshape(4, 4, 16, TN)
            at = (part, slice(None), slice(None), slice(None), cut(t))
            over[part, t] = send(f0s.at[at], f0r.at[at], sf0, part * 4 + t, sibling)

    def toward(part, t, i):
        if part == 0:
            return f1s.at[0, :, (x + 4 + i) % 4, :, cut(t)]
        return f1s.at[1, (y + 4 + i) % 4, :, :, cut(t)]

    plain, opposite, joined, final = {}, {}, {}, {}

    def way(part, t):
        axis = second_axis[part]
        return (1, axis[0], axis[2]) if t % 2 == 0 else (-1, axis[2], axis[0])

    def own_chunk(t):
        for part in range(2):
            over[part, t].wait_recv()
            both = down(core, part, t) + f0r[part, :, :, :, cut(t)].reshape(256, TN).astype(F32)
            f1s[part, :, :, :, cut(t)] = both.astype(BF16).reshape(4, 4, 16, TN)
            step, ahead, behind = way(part, t)
            k = (part * 4 + t) * 3
            opposite[part, t] = send(toward(part, t, 2), fo.at[part, :, :, cut(t)], sf1, k, ahead)
            plain[part, t] = send(toward(part, t, -step), fd.at[part, :, :, cut(t)], sf1, k + 1, behind)

    def join_chunk(t):
        for part in range(2):
            step, ahead, behind = way(part, t)
            opposite[part, t].wait_recv()
            fcs[part, :, :, cut(t)] = (
                toward(part, t, step)[...].astype(F32) + fo[part, :, :, cut(t)].astype(F32)
            ).astype(BF16)
            at = (part, slice(None), slice(None), cut(t))
            joined[part, t] = send(fcs.at[at], fcr.at[at], sf1, (part * 4 + t) * 3 + 2, ahead)

    def end_chunk(t):
        for part in range(2):
            plain[part, t].wait_recv()
            joined[part, t].wait_recv()
            f2s[part, :, :, cut(t)] = (
                toward(part, t, 0)[...].astype(F32)
                + fd[part, :, :, cut(t)].astype(F32)
                + fcr[part, :, :, cut(t)].astype(F32)
            ).astype(BF16)
            for k, (p, d) in enumerate((y_peers, x_peers)[part]):
                final[part, t, k] = send(
                    f2s.at[part, p, :, cut(t)], f2r.at[part, k, :, cut(t)], sf2, (part * 4 + t) * 3 + k, d
                )

    own_chunk(0)
    own_chunk(1)
    join_chunk(0)
    own_chunk(2)
    join_chunk(1)
    own_chunk(3)
    join_chunk(2)
    end_chunk(0)
    join_chunk(3)
    end_chunk(1)
    end_chunk(2)
    end_chunk(3)
    for sent in (over, plain, opposite, joined, final):
        pending += list(sent.values())
    for t in chunks:
        for part in range(2):
            for k in range(3):
                final[part, t, k].wait_recv()
            for j in range(t * 4, t * 4 + 4):
                at = slice(j * 128, j * 128 + 128)
                total = f2s[part, (y, x)[part], :, at].astype(F32)
                for k in range(3):
                    total = total + f2r[part, k, :, at].astype(F32)
                f3f[pl.ds(part * 16 + j, 16, stride=32), :] = total
    f3s[...] = f3f[...].astype(BF16)
    copies = [send(rows(f3s, p, 32), f3r.at[zc], sf3, k, d) for k, (p, d) in enumerate(zc_peers)]
    f3r[zc] = rows(f3s, zc, 32)[...]
    for c in copies:
        c.wait_recv()
    pending += copies
    low, high = f3r[0].astype(F32), f3r[1].astype(F32)
    for k in range(1, 8):
        low = low + f3r[2 * k].astype(F32)
        high = high + f3r[2 * k + 1].astype(F32)
    out_ref[...] = (hid[...] + jnp.concatenate([low, high], axis=0)).astype(BF16)
    for c in pending:
        c.wait_send()


def on_device(
    resid, query, fresh_kv, cache_home, kv_cache, cached_len, wo, norm_gain, w_router,
    expert_ids, w_gate, w_up, w_down,
):
    vmem, smem, hbm = (
        pl.BlockSpec(memory_space=pltpu.VMEM),
        pl.BlockSpec(memory_space=pltpu.SMEM),
        pl.BlockSpec(memory_space=pl.ANY),
    )
    v = pltpu.VMEM
    sem = lambda n: pltpu.SemaphoreType.DMA((2, n))
    out = pl.pallas_call(
        kernel,
        out_shape=jax.ShapeDtypeStruct((64, 128), BF16),
        in_specs=[vmem, smem, smem, vmem, vmem, vmem, vmem, vmem, hbm, hbm, hbm, hbm, hbm],
        out_specs=vmem,
        scratch_shapes=[
            v((128, 2048), BF16), v((128, 8192), BF16), v((2, 192, 8192), BF16), v((192, 8192), BF16),
            pltpu.SemaphoreType.DMA((5,)),
            v((128, 128), F32), v((128, 128), F32), v((128, 128), F32), v((128, 128), F32),
            v((64, 128), F32), v((64, 128), F32), v((64, 128), F32), v((64, 128), F32),
            v((8, 16, CZ // 2), BF16), v((7, 16, CZ // 2), BF16),
            v((8, 16, CX // 2), BF16), v((7, 16, CX // 2), BF16),
            v((8 * PZ, 128), BF16), v((7, PZ, 128), BF16), v((8 * PX, 128), BF16), v((7, PX, 128), BF16),
            v((8 * PZ, 128), F32), v((8 * PX, 128), F32), v((64, 128), F32), v((256, 128), F32),
            v((64, 128), BF16), v((512, 128), BF16), v((512, 128), F32),
            v((8, 128), F32), v((16, 8, 128), F32), v((4, 4, 16, 128), F32),
            v((2, 4, 4, 16, 2048), BF16), v((2, 4, 4, 16, 2048), BF16),
            v((2, 256, 192), F32), v((256, 192), BF16),
            v((2, 4, 4, 16, 2048), BF16), v((2, 4, 4, 16, 2048), BF16), v((2, 4, 4, 16, 2048), BF16),
            v((2, 4, 16, 2048), BF16), v((2, 4, 16, 2048), BF16), v((2, 4, 16, 2048), BF16), v((2, 4, 16, 2048), BF16),
            v((2, 4, 16, 2048), BF16), v((2, 3, 16, 2048), BF16),
            v((512, 128), F32), v((512, 128), BF16), v((16, 32, 128), BF16),
            sem(7), sem(7), sem(7), sem(7), sem(7), sem(7), sem(7), sem(7),
            sem(15), sem(21), sem(6), sem(24), sem(14), sem(8), sem(24), sem(24), sem(15),
        ],
        compiler_params=pltpu.CompilerParams(
            collective_id=0, has_side_effects=True, vmem_limit_bytes=60 * 2**20
        ),
    )(
        cache_home, cached_len, expert_ids, query, jnp.transpose(fresh_kv), resid,
        norm_gain.reshape(64, 128), jnp.transpose(w_router),
        kv_cache, wo, w_gate, w_up, w_down,
    )
    return out.reshape(1, 8192)


def solution(mesh):
    return jax.shard_map(
        on_device,
        mesh=mesh,
        in_specs=(
            P(("tier", "grp"), None),
            P("tier", "grp"),
            P("tier", "grp"),
            P("tier", None),
            P(("tier", "grp"), None, None),
            P(("tier", "grp")),
            P("grp", None),
            P(),
            P(),
            P(("tier", "grp"), None),
            P("tier", "grp", None),
            P("tier", "grp", None),
            P("tier", "grp", None),
        ),
        out_specs=P(("tier", "grp"), None),
        check_vma=False,
    )
```

```python
import functools
import math

import jax
import jax.numpy as jnp
from jax import lax
from jax.experimental import pallas as pl
from jax.experimental.pallas import tpu as pltpu
from jax.sharding import PartitionSpec as P

MESH = pl.DeviceIdType.MESH
F32 = jnp.float32
BF16 = jnp.bfloat16
CZ = 3072
CX = 8192 - CZ
SZ = CZ // 128
SX = CX // 128
PZ, PX = -(-SZ // 16) * 16, -(-SX // 16) * 16
TN = 512


def iota(shape, dim):
    return lax.broadcasted_iota(jnp.int32, shape, dim)


def nt(a, b):
    return lax.dot_general(a, b, (((1,), (1,)), ((), ())), preferred_element_type=F32)


def nn(a, b):
    return jnp.dot(a, b, preferred_element_type=F32)


def kernel(
    home_ref, len_ref, ids_ref, query_ref, fresh_ref, resid_hbm, gain_hbm, router_hbm,
    cache_hbm, wo_hbm, gate_hbm, up_hbm, down_hbm,
    out_ref,
    cache, wo, w_in, w_down, local_sem,
    resid, gain, router_in, a1s, a1r, a1f, a2s, a2r, c1s, c1r, c2s, c2r,
    r1zs, r1zr, r1xs, r1xr, r2zs, r2zr, r2xs, r2xr,
    r2fz, r2fx, hid, router,
    g1s, g1r, g1f, gates, gate_in, gate_all, xa, xb, acc, act,
    f0s, f0r, f1s, fo, fd, fcs, fcr, f2s, f2r, f3f, f3s, f3r,
    sa1, sa2, sc1, sc2, sr1z, sr1x, sr2z, sr2x, sg1, sgate, sg2, sg3, sg4, sf0, sf1, sf2, sf3,
):
    tier, grp = lax.axis_index("tier"), lax.axis_index("grp")
    y_hi, core = tier // 2, tier % 2
    y_lo, z, x = grp // 32, (grp // 4) % 8, grp % 4
    y = y_hi * 2 + y_lo
    xy = y_lo * 4 + x
    zc = z * 2 + core

    def device(y, z, x, core):
        return ((y // 2) * 2 + core, (y % 2) * 32 + z * 4 + x)

    def send(src, dst, sems, k, to):
        copy = pltpu.make_async_remote_copy(
            src_ref=src, dst_ref=dst, send_sem=sems.at[0, k], recv_sem=sems.at[1, k],
            device_id=to, device_id_type=MESH,
        )
        copy.start()
        return copy

    far_first = (4, 3, 5, 2, 6, 1, 7)
    z_peers = [((z + k) % 8, device(y, (z + k) % 8, x, core)) for k in far_first]
    xy_peers = []
    for k_lo, k in ((1, 2), (0, 2), (1, 1), (1, 3), (0, 1), (0, 3), (1, 0)):
        px, p_lo = (x + k) % 4, (y_lo + k_lo) % 2
        xy_peers.append((p_lo * 4 + px, device(y_hi * 2 + p_lo, z, px, core)))
    zc_peers = []
    for k in far_first + (0,):
        for k_core in (1, 0)[: 2 if k else 1]:
            pz, pc = (z + k) % 8, (core + k_core) % 2
            zc_peers.append((pz * 2 + pc, device(y, pz, x, pc)))

    x_peers = [((x + k) % 4, device(y, z, (x + k) % 4, core)) for k in range(1, 4)]
    y_peers = [((y + k) % 4, device((y + k) % 4, z, x, core)) for k in range(1, 4)]
    sibling = device(y, z, x, 1 - core)
    far = [device(((1 - y_hi) * 2 + (y_lo + k) % 2), z, x, core) for k in range(2)]

    loads = [
        pltpu.make_async_copy(cache_hbm.at[0], cache, local_sem.at[0]),
        pltpu.make_async_copy(wo_hbm, wo, local_sem.at[1]),
        pltpu.make_async_copy(gate_hbm.at[0], w_in.at[0], local_sem.at[2]),
        pltpu.make_async_copy(up_hbm.at[0], w_in.at[1], local_sem.at[3]),
        pltpu.make_async_copy(down_hbm.at[0], w_down, local_sem.at[4]),
        pltpu.make_async_copy(resid_hbm, resid, local_sem.at[5]),
        pltpu.make_async_copy(gain_hbm, gain, local_sem.at[6]),
        pltpu.make_async_copy(router_hbm, router_in, local_sem.at[7]),
    ]
    barrier = pltpu.get_barrier_semaphore()
    greeted = [d for _, d in zc_peers] + [d for _, d in xy_peers] + far
    for d in greeted:
        pl.semaphore_signal(barrier, inc=1, device_id=d, device_id_type=MESH)

    slot = home_ref[...]
    place = ((slot >> 2) & 7) * 8 + (slot >> 5) * 4 + (slot & 3)
    to_slot = (iota((64, 64), 0) == place).astype(BF16)
    spread_fresh = (iota((32, 128), 1) == iota((32, 128), 0) + 32 * x).astype(BF16)
    by_slot_q = nn(to_slot, query_ref[...])
    by_slot_f = nn(nt(to_slot, fresh_ref[...]).astype(BF16), spread_fresh)
    for k in range(8):
        a1s[k * 16 : k * 16 + 16] = jnp.concatenate(
            [by_slot_q[k * 8 : k * 8 + 8], by_slot_f[k * 8 : k * 8 + 8]], axis=0
        ).astype(BF16)

    pl.semaphore_wait(barrier, len(greeted))

    def rows(ref, i, n):
        return ref.at[pl.ds(pl.multiple_of(i * n, n), n)]

    pending = []
    copies = [
        send(rows(a1s, p, 16), rows(a1r, z, 16), sa1, k, d) for k, (p, d) in enumerate(z_peers)
    ]
    rows(a1r, z, 16)[...] = rows(a1s, z, 16)[...]
    for load in loads[5:] + loads[:5]:
        load.start()
    r2fz[...] = jnp.zeros_like(r2fz)
    r2fx[...] = jnp.zeros_like(r2fx)
    for c in copies:
        c.wait_recv()
    pending += copies
    a1f[...] = a1r[...].astype(F32)
    for k in range(8):
        a2s[k * 16 : k * 16 + 16] = jnp.concatenate(
            [a1f[pl.ds(k, 8, stride=16), :], a1f[pl.ds(8 + k, 8, stride=16), :]], axis=0
        ).astype(BF16)
    copies = [
        send(rows(a2s, p, 16), rows(a2r, xy, 16), sa2, k, d) for k, (p, d) in enumerate(xy_peers)
    ]
    rows(a2r, xy, 16)[...] = rows(a2s, xy, 16)[...]
    for load in loads[5:]:
        load.wait()
    resid_row, router_rows = resid[...].astype(F32), router_in[...].astype(F32)
    for j in range(64):
        hid[j : j + 1] = resid_row[:, j * 128 : j * 128 + 128]
        router[pl.ds(j, 4, stride=64), :] = router_rows[:, j * 128 : j * 128 + 128]
    for c in copies:
        c.wait_recv()
    pending += copies

    head = iota((64, 128), 0)
    group = (head >> 5) * 4 + ((head & 7) >> 1)
    got = a2r[...].astype(F32).reshape(8, 16, 128)
    queries = got[:, :8].reshape(64, 128)
    news = got[:, 8:]
    new_key = (news[0] + news[1] + news[2] + news[3]).astype(BF16)
    new_value = (news[4] + news[5] + news[6] + news[7]).astype(BF16)
    of_group = (iota((64, 8), 1) == (iota((64, 8), 0) >> 5) * 4 + ((iota((64, 8), 0) & 7) >> 1)).astype(BF16)
    own_key = nn(of_group, new_key)
    own_value = nn(of_group, new_value)
    loads[0].wait()
    wide = jnp.concatenate(
        [jnp.where(group == j, queries, 0.0).astype(BF16) for j in range(8)], axis=1
    )
    scale = 1.0 / math.sqrt(128)
    scores = nt(wide, cache[:, :1024]) * scale
    scores = jnp.where(iota((64, 128), 1) < len_ref[0], scores, -1e30)
    own_score = jnp.sum(queries * own_key, axis=1, keepdims=True) * scale
    top = jnp.maximum(jnp.max(scores, axis=1, keepdims=True), own_score)
    weights = jnp.exp(scores - top)
    own_weight = jnp.exp(own_score - top)
    denominator = jnp.sum(weights, axis=1, keepdims=True) + own_weight
    weights = (weights / denominator).astype(BF16)
    own_weight = (own_weight / denominator).astype(BF16).astype(F32)
    mixed = nn(weights, cache[:, 1024:])
    outcome = own_weight * own_value
    for j in range(8):
        outcome = outcome + jnp.where(group == j, mixed[:, j * 128 : (j + 1) * 128], 0.0)
    c1s[...] = outcome.astype(BF16).astype(F32)

    copies = [
        send(rows(c1s, p, 8), rows(c1r, xy, 8), sc1, k, d) for k, (p, d) in enumerate(xy_peers)
    ]
    rows(c1r, xy, 8)[...] = rows(c1s, xy, 8)[...]
    for c in copies:
        c.wait_recv()
    pending += copies
    for k in range(8):
        c2s[k * 8 : k * 8 + 8] = c1r[pl.ds(k, 8, stride=8), :]
    copies = [
        send(rows(c2s, p, 8), rows(c2r, z, 8), sc2, k, d) for k, (p, d) in enumerate(z_peers)
    ]
    rows(c2r, z, 8)[...] = rows(c2s, z, 8)[...]
    for c in copies:
        c.wait_recv()
    pending += copies

    own = iota((64, 64), 1)
    own_z, own_xy = (own >> 2) & 7, (own >> 5) * 4 + (own & 3)
    by_head = c2r[...].astype(BF16)
    order_z = (iota((64, 64), 0) == own_z * 8 + own_xy).astype(BF16)
    order_x = (iota((64, 64), 0) == own_xy * 8 + own_z).astype(BF16)
    att_z = nn(nt(order_z, to_slot).astype(BF16), by_head).astype(BF16)
    att_x = nn(nt(order_x, to_slot).astype(BF16), by_head).astype(BF16)
    loads[1].wait()

    def project(att, ref, base, width):
        def tile(t, _):
            at = pl.multiple_of(t * TN, TN)
            lo = nn(att, wo[:, pl.ds(base + at, TN)]).reshape(8, 8, TN)
            hi = nn(att, wo[:, pl.ds(base + width + at, TN)]).reshape(8, 8, TN)
            ref[:, :, pl.ds(at, TN)] = jnp.concatenate([lo, hi], axis=1).astype(BF16)
            return 0

        lax.fori_loop(0, width // TN, tile, 0)

    project(att_z, r1zs, 0, CZ // 2)
    copies_z = [send(r1zs.at[p], r1zr.at[k], sr1z, k, d) for k, (p, d) in enumerate(z_peers)]
    project(att_x, r1xs, CZ, CX // 2)
    copies_x = [send(r1xs.at[p], r1xr.at[k], sr1x, k, d) for k, (p, d) in enumerate(xy_peers)]
    pending += copies_z + copies_x

    def fold(sent, mine, received, n, slabs, used, stride):
        def tile(j, _):
            at = pl.multiple_of(j * 128, 128)
            total = sent[mine, :, pl.ds(at, 128)].astype(F32)
            for k in range(n):
                total = total + received[k, :, pl.ds(at, 128)].astype(F32)
            slabs[pl.ds(j, 8, stride=stride), :] = total[:8]
            slabs[pl.ds(j + used // 2, 8, stride=stride), :] = total[8:]
            return 0

        lax.fori_loop(0, used // 2, tile, 0)

    for c in copies_z:
        c.wait_recv()
    fold(r1zs, z, r1zr, 7, r2fz, SZ, PZ)
    r2zs[...] = r2fz[...].astype(BF16)
    copies_z = [
        send(rows(r2zs, p, PZ), r2zr.at[k], sr2z, k, d) for k, (p, d) in enumerate(xy_peers)
    ]
    for c in copies_x:
        c.wait_recv()
    fold(r1xs, xy, r1xr, 7, r2fx, SX, PX)
    r2xs[...] = r2fx[...].astype(BF16)
    copies_x = [
        send(rows(r2xs, p, PX), r2xr.at[k], sr2x, k, d) for k, (p, d) in enumerate(z_peers)
    ]
    for c in copies_z + copies_x:
        c.wait_recv()
    pending += copies_z + copies_x
    part_z, part_x = rows(r2fz, xy, PZ)[...], rows(r2fx, z, PX)[...]
    for k in range(7):
        part_z = part_z + r2zr[k].astype(F32)
        part_x = part_x + r2xr[k].astype(F32)
    hidden = hid[...] + jnp.concatenate([part_z[:SZ], part_x[:SX]], axis=0)
    hid[...] = hidden

    mean = jnp.sum(hidden * hidden, keepdims=True) * (1.0 / 8192)
    normed = (hidden * lax.rsqrt(mean + 1e-05) * gain[...].astype(F32)).astype(BF16)
    normed_wide = normed.astype(F32)
    logits = [
        jnp.sum(normed_wide * router[e * 64 : e * 64 + 64], keepdims=True) for e in range(4)
    ]
    first, second = ids_ref[0, 0], ids_ref[0, 1]
    zero = jnp.zeros((1, 1), F32)
    logit_a, logit_b = zero, zero
    for e in range(4):
        logit_a = logit_a + jnp.where(first == e, logits[e], zero)
        logit_b = logit_b + jnp.where(second == e, logits[e], zero)
    gate_a = 1.0 / (1.0 + jnp.exp(logit_b - logit_a))
    gate_b = 1.0 / (1.0 + jnp.exp(logit_a - logit_b))
    lane = iota((8, 128), 1)
    gates[...] = jnp.where(lane == first, gate_a, 0.0) + jnp.where(lane == second, gate_b, 0.0)
    g1s[...] = normed

    halves = [
        [
            send(rows(g1s, p % 2 * 2 + part, 16), rows(g1r, part * 16 + zc, 16), sg1, part * 15 + k, d)
            for k, (p, d) in enumerate(zc_peers)
        ]
        for part in range(2)
    ]
    gate_copies = [
        send(gates.at[pl.ds(0, 1)], gate_in.at[zc, pl.ds(0, 1)], sgate, k, d)
        for k, (p, d) in enumerate(zc_peers)
    ]
    for part in range(2):
        rows(g1r, part * 16 + zc, 16)[...] = rows(g1s, core * 2 + part, 16)[...]
    gate_in[zc] = gates[...]
    pending += halves[0] + halves[1] + gate_copies

    def block(part, j, i):
        if part == 0:
            return xa.at[core, (y + 4 - j) % 4, (x + 4 - i) % 4]
        return xb.at[core, (y + 4 - i) % 4, (x + 4 - j) % 4]

    def line(part, i):
        if part == 0:
            return xa.at[core, :, (x + 4 - i) % 4]
        return xb.at[core, (y + 4 - i) % 4]

    first_axis = [[d for _, d in y_peers], [d for _, d in x_peers]]
    second_axis = [[d for _, d in x_peers], [d for _, d in y_peers]]
    across = []
    middle = [{}, {}]
    onward = [{}, {}]

    def pass_on(part, j):
        ref = block(part, j, 0)
        for to, k in ((0, 0), (2, 4)):
            onward[part][k + j] = send(ref, ref, sg3, part * 12 + k + j, second_axis[part][to])
        if j == 2:
            onward[part][10] = send(ref, ref, sg3, part * 12 + 10, second_axis[part][1])
        across.append(send(ref, ref, sg4, part * 10 + j, sibling))

    def relay(part, j):
        if j % 2 == 0:
            onward[part][j].wait_recv()
            ref, to = block(part, j, 1), second_axis[part][0]
        else:
            onward[part][4 + j].wait_recv()
            ref, to = block(part, j, 3), second_axis[part][2]
        onward[part][8 + j] = send(ref, ref, sg3, part * 12 + 8 + j, to)

    for part in range(2):
        for c in halves[part]:
            c.wait_recv()
        g1f[...] = rows(g1r, part, 256)[...].astype(F32)
        for j in range(16):
            block(part, 0, 0)[:, j * 128 : j * 128 + 128] = g1f[pl.ds(j, 16, stride=16), :].astype(BF16)
        ref = block(part, 0, 0)
        for k in (1, 0, 2):
            middle[part][k] = send(ref, ref, sg2, part * 3 + k, first_axis[part][k])
        pass_on(part, 0)
    for j in (1, 3):
        for part in range(2):
            middle[part][j - 1].wait_recv()
            pass_on(part, j)
    for part in range(2):
        relay(part, 0)
    for part in range(2):
        middle[part][1].wait_recv()
        pass_on(part, 2)
    for j in (1, 3):
        for part in range(2):
            relay(part, j)
    for c in gate_copies:
        c.wait_recv()
    for i in range(16):
        gate_all[y, x, i : i + 1] = gate_in[i, 0:1]
    ref = gate_all.at[y, x]
    gate_middle = [send(ref, ref, sgate, 15 + k, d) for k, d in enumerate(first_axis[0])]
    for part in range(2):
        for j in (1, 2, 3):
            onward[part][j].wait_recv()
        across.append(send(line(part, 1), line(part, 1), sg4, part * 10 + 4, sibling))
        for j in (0, 2):
            onward[part][4 + j].wait_recv()
        across.append(send(line(part, 3), line(part, 3), sg4, part * 10 + 5, sibling))
    for c in gate_middle:
        c.wait_recv()
    ref = gate_all.at[:, x]
    gate_onward = [send(ref, ref, sgate, 18 + k, d) for k, d in enumerate(second_axis[0])]
    for part in range(2):
        for j in (0, 1, 3, 2):
            onward[part][8 + j].wait_recv()
            across.append(send(block(part, j, 2), block(part, j, 2), sg4, part * 10 + 6 + j, sibling))
    pending += across + gate_middle + gate_onward
    for part in range(2):
        pending += list(middle[part].values()) + list(onward[part].values())

    for load in loads[2:5]:
        load.wait()
    acc[...] = jnp.zeros_like(acc)

    def into(half):
        def tile(t, _):
            at = pl.multiple_of(t * TN, TN)
            for part, ref in ((0, xa), (1, xb)):
                rows_in = ref[half, :, :, :, pl.ds(at, TN)].reshape(256, TN)
                column = pl.ds(pl.multiple_of(half * 4096 + part * 2048 + at, TN), TN)
                acc[0] += nt(rows_in, w_in[0, :, column])
                acc[1] += nt(rows_in, w_in[1, :, column])
            return 0

        lax.fori_loop(0, 2048 // TN, tile, 0)

    into(core)
    for c in across:
        c.wait_recv()
    into(1 - core)
    gate_part = acc[0]
    act[...] = (gate_part / (1.0 + jnp.exp(-gate_part)) * acc[1]).astype(BF16)
    for c in gate_onward:
        c.wait_recv()
    mine = iota((256, 128), 1) == tier
    gate = jnp.sum(jnp.where(mine, gate_all[...].reshape(256, 128), 0.0), axis=1, keepdims=True)

    def down(half, part, t):
        column = pl.ds(pl.multiple_of(half * 4096 + part * 2048 + t * TN, TN), TN)
        return nn(act[...], w_down[:, column]) * gate

    chunks = range(4)

    def cut(t):
        return slice(t * TN, t * TN + TN)

    over = {}
    for t in chunks:
        for part in range(2):
            f0s[part, :, :, :, cut(t)] = down(1 - core, part, t).astype(BF16).reshape(4, 4, 16, TN)
            at = (part, slice(None), slice(None), slice(None), cut(t))
            over[part, t] = send(f0s.at[at], f0r.at[at], sf0, part * 4 + t, sibling)

    def toward(part, t, i):
        if part == 0:
            return f1s.at[0, :, (x + 4 + i) % 4, :, cut(t)]
        return f1s.at[1, (y + 4 + i) % 4, :, :, cut(t)]

    plain, opposite, joined, final = {}, {}, {}, {}

    def way(part, t):
        axis = second_axis[part]
        return (1, axis[0], axis[2]) if t % 2 == 0 else (-1, axis[2], axis[0])

    def own_chunk(t):
        for part in range(2):
            over[part, t].wait_recv()
            both = down(core, part, t) + f0r[part, :, :, :, cut(t)].reshape(256, TN).astype(F32)
            f1s[part, :, :, :, cut(t)] = both.astype(BF16).reshape(4, 4, 16, TN)
            step, ahead, behind = way(part, t)
            k = (part * 4 + t) * 3
            if t == 3:
                axis = second_axis[part]
                at = (part, slice(None), slice(None), cut(t))
                opposite[part, t] = send(toward(part, t, 2), fo.at[at], sf1, k, axis[1])
                plain[part, t] = send(toward(part, t, 1), fd.at[at], sf1, k + 1, axis[0])
                joined[part, t] = send(toward(part, t, 3), fcr.at[at], sf1, k + 2, axis[2])
                continue
            opposite[part, t] = send(toward(part, t, 2), fo.at[part, :, :, cut(t)], sf1, k, ahead)
            plain[part, t] = send(toward(part, t, -step), fd.at[part, :, :, cut(t)], sf1, k + 1, behind)

    def join_chunk(t):
        for part in range(2):
            step, ahead, behind = way(part, t)
            opposite[part, t].wait_recv()
            fcs[part, :, :, cut(t)] = (
                toward(part, t, step)[...].astype(F32) + fo[part, :, :, cut(t)].astype(F32)
            ).astype(BF16)
            at = (part, slice(None), slice(None), cut(t))
            joined[part, t] = send(fcs.at[at], fcr.at[at], sf1, (part * 4 + t) * 3 + 2, ahead)

    def end_chunk(t):
        for part in range(2):
            plain[part, t].wait_recv()
            joined[part, t].wait_recv()
            total = (
                toward(part, t, 0)[...].astype(F32)
                + fd[part, :, :, cut(t)].astype(F32)
                + fcr[part, :, :, cut(t)].astype(F32)
            )
            if t == 3:
                opposite[part, t].wait_recv()
                total = total + fo[part, :, :, cut(t)].astype(F32)
            f2s[part, :, :, cut(t)] = total.astype(BF16)
            for k, (p, d) in enumerate((y_peers, x_peers)[part]):
                final[part, t, k] = send(
                    f2s.at[part, p, :, cut(t)], f2r.at[part, k, :, cut(t)], sf2, (part * 4 + t) * 3 + k, d
                )

    last = {}

    def finish_chunk(t):
        half = t // 2
        for part in range(2):
            for k in range(3):
                final[part, t, k].wait_recv()
            for j in range(4):
                at = slice((t * 4 + j) * 128, (t * 4 + j + 1) * 128)
                total = f2s[part, (y, x)[part], :, at].astype(F32)
                for k in range(3):
                    total = total + f2r[part, k, :, at].astype(F32)
                f3f[pl.ds(half * 256 + part * 8 + t % 2 * 4 + j, 16, stride=16), :] = total
        if t % 2 == 1:
            rows(f3s, half, 256)[...] = rows(f3f, half, 256)[...].astype(BF16)
            for k, (p, d) in enumerate(zc_peers):
                last[half, k] = send(rows(f3s, half * 16 + p, 16), f3r.at[half, zc], sf3, half * 15 + k, d)
            f3r[half, zc] = rows(f3s, half * 16 + zc, 16)[...]

    own_chunk(0)
    own_chunk(1)
    join_chunk(0)
    own_chunk(2)
    join_chunk(1)
    own_chunk(3)
    join_chunk(2)
    end_chunk(0)
    end_chunk(1)
    end_chunk(2)
    finish_chunk(0)
    end_chunk(3)
    finish_chunk(1)
    finish_chunk(2)
    finish_chunk(3)
    for sent in (over, plain, opposite, joined, final, last):
        pending += list(sent.values())
    for c in last.values():
        c.wait_recv()
    sums = []
    for c in range(2):
        parts = []
        for half in range(2):
            total = f3r[half, c].astype(F32)
            for k in range(1, 8):
                total = total + f3r[half, 2 * k + c].astype(F32)
            parts.append(total)
        sums += [parts[0][:8], parts[1][:8], parts[0][8:], parts[1][8:]]
    out_ref[...] = (hid[...] + jnp.concatenate(sums, axis=0)).astype(BF16)
    for c in pending:
        c.wait_send()


def on_device(
    resid, query, fresh_kv, cache_home, kv_cache, cached_len, wo, norm_gain, w_router,
    expert_ids, w_gate, w_up, w_down,
):
    vmem, smem, hbm = (
        pl.BlockSpec(memory_space=pltpu.VMEM),
        pl.BlockSpec(memory_space=pltpu.SMEM),
        pl.BlockSpec(memory_space=pl.ANY),
    )
    v = pltpu.VMEM
    sem = lambda n: pltpu.SemaphoreType.DMA((2, n))
    out = pl.pallas_call(
        kernel,
        out_shape=jax.ShapeDtypeStruct((64, 128), BF16),
        in_specs=[vmem, smem, smem, vmem, vmem] + [hbm] * 8,
        out_specs=vmem,
        scratch_shapes=[
            v((128, 2048), BF16), v((128, 8192), BF16), v((2, 192, 8192), BF16), v((192, 8192), BF16),
            pltpu.SemaphoreType.DMA((8,)),
            v((1, 8192), BF16), v((64, 128), BF16), v((4, 8192), BF16),
            v((128, 128), BF16), v((128, 128), BF16), v((128, 128), F32), v((128, 128), BF16), v((128, 128), BF16),
            v((64, 128), F32), v((64, 128), F32), v((64, 128), F32), v((64, 128), F32),
            v((8, 16, CZ // 2), BF16), v((7, 16, CZ // 2), BF16),
            v((8, 16, CX // 2), BF16), v((7, 16, CX // 2), BF16),
            v((8 * PZ, 128), BF16), v((7, PZ, 128), BF16), v((8 * PX, 128), BF16), v((7, PX, 128), BF16),
            v((8 * PZ, 128), F32), v((8 * PX, 128), F32), v((64, 128), F32), v((256, 128), F32),
            v((64, 128), BF16), v((512, 128), BF16), v((256, 128), F32),
            v((8, 128), F32), v((16, 8, 128), F32), v((4, 4, 16, 128), F32),
            v((2, 4, 4, 16, 2048), BF16), v((2, 4, 4, 16, 2048), BF16),
            v((2, 256, 192), F32), v((256, 192), BF16),
            v((2, 4, 4, 16, 2048), BF16), v((2, 4, 4, 16, 2048), BF16), v((2, 4, 4, 16, 2048), BF16),
            v((2, 4, 16, 2048), BF16), v((2, 4, 16, 2048), BF16), v((2, 4, 16, 2048), BF16), v((2, 4, 16, 2048), BF16),
            v((2, 4, 16, 2048), BF16), v((2, 3, 16, 2048), BF16),
            v((512, 128), F32), v((512, 128), BF16), v((2, 16, 16, 128), BF16),
            sem(7), sem(7), sem(7), sem(7), sem(7), sem(7), sem(7), sem(7),
            sem(30), sem(21), sem(6), sem(24), sem(20), sem(8), sem(24), sem(24), sem(30),
        ],
        compiler_params=pltpu.CompilerParams(
            collective_id=0, has_side_effects=True, vmem_limit_bytes=60 * 2**20
        ),
    )(
        cache_home, cached_len, expert_ids, query, jnp.transpose(fresh_kv), resid,
        norm_gain.reshape(64, 128), jnp.transpose(w_router),
        kv_cache, wo, w_gate, w_up, w_down,
    )
    return out.reshape(1, 8192)


def solution(mesh):
    return jax.shard_map(
        on_device,
        mesh=mesh,
        in_specs=(
            P(("tier", "grp"), None),
            P("tier", "grp"),
            P("tier", "grp"),
            P("tier", None),
            P(("tier", "grp"), None, None),
            P(("tier", "grp")),
            P("grp", None),
            P(),
            P(),
            P(("tier", "grp"), None),
            P("tier", "grp", None),
            P("tier", "grp", None),
            P("tier", "grp", None),
        ),
        out_specs=P(("tier", "grp"), None),
        check_vma=False,
    )
```

```python
import functools
import math

import jax
import jax.numpy as jnp
from jax import lax
from jax.experimental import pallas as pl
from jax.experimental.pallas import tpu as pltpu
from jax.sharding import PartitionSpec as P

MESH = pl.DeviceIdType.MESH
F32 = jnp.float32
BF16 = jnp.bfloat16
WZ = 768
WX = 2048 - WZ
SZ, SX = 2 * WZ // 128, 2 * WX // 128
PZ, PX = -(-SZ // 16) * 16, -(-SX // 16) * 16
TN = 512


def iota(shape, dim):
    return lax.broadcasted_iota(jnp.int32, shape, dim)


def nt(a, b):
    return lax.dot_general(a, b, (((1,), (1,)), ((), ())), preferred_element_type=F32)


def nn(a, b):
    return jnp.dot(a, b, preferred_element_type=F32)


def kernel(
    home_ref, len_ref, ids_ref, query_ref, fresh_ref, resid_hbm, gain_hbm, router_hbm,
    cache_hbm, wo_hbm, gate_hbm, up_hbm, down_hbm,
    out_ref,
    cache, wo, w_in, w_down, local_sem,
    resid, gain, router_in, a1s, a1r, a1f, a2s, a2r, c1s, c1r, c2s, c2r,
    r1zs, r1zr, r1xs, r1xr, r2zs, r2zr, r2xs, r2xr,
    r2fz, r2fx, hid, router,
    g1s, g1r, g1f, gates, gate_in, gate_all, xa, xb, acc, act,
    f0s, f0r, f1s, fo, fd, fcs, fcr, f2s, f2r, f3f, f3s, f3r,
    sa1, sa2, sc1, sc2, sr1z, sr1x, sr2z, sr2x, sg1, sgate, sg2, sg3, sg4, sf0, sf1, sf2, sf3,
):
    tier, grp = lax.axis_index("tier"), lax.axis_index("grp")
    y_hi, core = tier // 2, tier % 2
    y_lo, z, x = grp // 32, (grp // 4) % 8, grp % 4
    y = y_hi * 2 + y_lo
    xy = y_lo * 4 + x
    zc = z * 2 + core

    def device(y, z, x, core):
        return ((y // 2) * 2 + core, (y % 2) * 32 + z * 4 + x)

    def send(src, dst, sems, k, to):
        copy = pltpu.make_async_remote_copy(
            src_ref=src, dst_ref=dst, send_sem=sems.at[0, k], recv_sem=sems.at[1, k],
            device_id=to, device_id_type=MESH,
        )
        copy.start()
        return copy

    far_first = (4, 3, 5, 2, 6, 1, 7)
    z_peers = [((z + k) % 8, device(y, (z + k) % 8, x, core)) for k in far_first]
    xy_peers = []
    for k_lo, k in ((1, 2), (0, 2), (1, 1), (1, 3), (0, 1), (0, 3), (1, 0)):
        px, p_lo = (x + k) % 4, (y_lo + k_lo) % 2
        xy_peers.append((p_lo * 4 + px, device(y_hi * 2 + p_lo, z, px, core)))
    zc_peers = []
    for k in far_first + (0,):
        for k_core in (1, 0)[: 2 if k else 1]:
            pz, pc = (z + k) % 8, (core + k_core) % 2
            zc_peers.append((pz * 2 + pc, device(y, pz, x, pc)))

    x_peers = [((x + k) % 4, device(y, z, (x + k) % 4, core)) for k in range(1, 4)]
    y_peers = [((y + k) % 4, device((y + k) % 4, z, x, core)) for k in range(1, 4)]
    sibling = device(y, z, x, 1 - core)
    far = [device(((1 - y_hi) * 2 + (y_lo + k) % 2), z, x, core) for k in range(2)]

    loads = [
        pltpu.make_async_copy(cache_hbm.at[0], cache, local_sem.at[0]),
        pltpu.make_async_copy(wo_hbm, wo, local_sem.at[1]),
        pltpu.make_async_copy(gate_hbm.at[0], w_in.at[0], local_sem.at[2]),
        pltpu.make_async_copy(up_hbm.at[0], w_in.at[1], local_sem.at[3]),
        pltpu.make_async_copy(down_hbm.at[0], w_down, local_sem.at[4]),
        pltpu.make_async_copy(resid_hbm, resid, local_sem.at[5]),
        pltpu.make_async_copy(gain_hbm, gain, local_sem.at[6]),
        pltpu.make_async_copy(router_hbm, router_in, local_sem.at[7]),
    ]
    barrier = pltpu.get_barrier_semaphore()
    greeted = [d for _, d in zc_peers] + [d for _, d in xy_peers] + far
    for d in greeted:
        pl.semaphore_signal(barrier, inc=1, device_id=d, device_id_type=MESH)

    slot = home_ref[...]
    place = ((slot >> 2) & 7) * 8 + (slot >> 5) * 4 + (slot & 3)
    to_slot = (iota((64, 64), 0) == place).astype(BF16)
    spread_fresh = (iota((32, 128), 1) == iota((32, 128), 0) + 32 * x).astype(BF16)
    by_slot_q = nn(to_slot, query_ref[...])
    by_slot_f = nn(nt(to_slot, fresh_ref[...]).astype(BF16), spread_fresh)
    for k in range(8):
        a1s[k * 16 : k * 16 + 16] = jnp.concatenate(
            [by_slot_q[k * 8 : k * 8 + 8], by_slot_f[k * 8 : k * 8 + 8]], axis=0
        ).astype(BF16)

    pl.semaphore_wait(barrier, len(greeted))

    def rows(ref, i, n):
        return ref.at[pl.ds(pl.multiple_of(i * n, n), n)]

    pending = []
    copies = [
        send(rows(a1s, p, 16), rows(a1r, z, 16), sa1, k, d) for k, (p, d) in enumerate(z_peers)
    ]
    rows(a1r, z, 16)[...] = rows(a1s, z, 16)[...]
    for load in loads[5:] + loads[:5]:
        load.start()
    r2fz[...] = jnp.zeros_like(r2fz)
    r2fx[...] = jnp.zeros_like(r2fx)
    for c in copies:
        c.wait_recv()
    pending += copies
    a1f[...] = a1r[...].astype(F32)
    for k in range(8):
        a2s[k * 16 : k * 16 + 16] = jnp.concatenate(
            [a1f[pl.ds(k, 8, stride=16), :], a1f[pl.ds(8 + k, 8, stride=16), :]], axis=0
        ).astype(BF16)
    copies = [
        send(rows(a2s, p, 16), rows(a2r, xy, 16), sa2, k, d) for k, (p, d) in enumerate(xy_peers)
    ]
    rows(a2r, xy, 16)[...] = rows(a2s, xy, 16)[...]
    for load in loads[5:]:
        load.wait()
    resid_row, router_rows = resid[...].astype(F32), router_in[...].astype(F32)
    for j in range(64):
        hid[j : j + 1] = resid_row[:, j * 128 : j * 128 + 128]
        router[pl.ds(j, 4, stride=64), :] = router_rows[:, j * 128 : j * 128 + 128]
    for c in copies:
        c.wait_recv()
    pending += copies

    head = iota((64, 128), 0)
    group = (head >> 5) * 4 + ((head & 7) >> 1)
    got = a2r[...].astype(F32).reshape(8, 16, 128)
    queries = got[:, :8].reshape(64, 128)
    news = got[:, 8:]
    new_key = (news[0] + news[1] + news[2] + news[3]).astype(BF16)
    new_value = (news[4] + news[5] + news[6] + news[7]).astype(BF16)
    of_group = (iota((64, 8), 1) == (iota((64, 8), 0) >> 5) * 4 + ((iota((64, 8), 0) & 7) >> 1)).astype(BF16)
    own_key = nn(of_group, new_key)
    own_value = nn(of_group, new_value)
    loads[0].wait()
    wide = jnp.concatenate(
        [jnp.where(group == j, queries, 0.0).astype(BF16) for j in range(8)], axis=1
    )
    scale = 1.0 / math.sqrt(128)
    scores = nt(wide, cache[:, :1024]) * scale
    scores = jnp.where(iota((64, 128), 1) < len_ref[0], scores, -1e30)
    own_score = jnp.sum(queries * own_key, axis=1, keepdims=True) * scale
    top = jnp.maximum(jnp.max(scores, axis=1, keepdims=True), own_score)
    weights = jnp.exp(scores - top)
    own_weight = jnp.exp(own_score - top)
    denominator = jnp.sum(weights, axis=1, keepdims=True) + own_weight
    weights = (weights / denominator).astype(BF16)
    own_weight = (own_weight / denominator).astype(BF16).astype(F32)
    mixed = nn(weights, cache[:, 1024:])
    outcome = own_weight * own_value
    for j in range(8):
        outcome = outcome + jnp.where(group == j, mixed[:, j * 128 : (j + 1) * 128], 0.0)
    c1s[...] = outcome.astype(BF16).astype(F32)

    copies = [
        send(rows(c1s, p, 8), rows(c1r, xy, 8), sc1, k, d) for k, (p, d) in enumerate(xy_peers)
    ]
    rows(c1r, xy, 8)[...] = rows(c1s, xy, 8)[...]
    for c in copies:
        c.wait_recv()
    pending += copies
    for k in range(8):
        c2s[k * 8 : k * 8 + 8] = c1r[pl.ds(k, 8, stride=8), :]
    copies = [
        send(rows(c2s, p, 8), rows(c2r, z, 8), sc2, k, d) for k, (p, d) in enumerate(z_peers)
    ]
    rows(c2r, z, 8)[...] = rows(c2s, z, 8)[...]
    for c in copies:
        c.wait_recv()
    pending += copies

    own = iota((64, 64), 1)
    own_z, own_xy = (own >> 2) & 7, (own >> 5) * 4 + (own & 3)
    by_head = c2r[...].astype(BF16)
    order_z = (iota((64, 64), 0) == own_z * 8 + own_xy).astype(BF16)
    order_x = (iota((64, 64), 0) == own_xy * 8 + own_z).astype(BF16)
    att_z = nn(nt(order_z, to_slot).astype(BF16), by_head).astype(BF16)
    att_x = nn(nt(order_x, to_slot).astype(BF16), by_head).astype(BF16)
    loads[1].wait()

    def project(att, ref, base, width):
        for at in range(0, width, width // 2):
            cut = slice(at, at + width // 2)
            lo = nn(att, wo[:, base + at : base + at + width // 2]).reshape(8, 8, width // 2)
            hi = nn(att, wo[:, 4096 + base + at : 4096 + base + at + width // 2]).reshape(8, 8, width // 2)
            ref[:, :, cut] = jnp.concatenate([lo, hi], axis=1).astype(BF16)

    def fold(sent, mine, received, slabs, base, used, stride):
        for j in range(used // 2):
            at = slice(j * 128, j * 128 + 128)
            total = sent[mine, :, at].astype(F32)
            for k in range(7):
                total = total + received[k, :, at].astype(F32)
            slabs[pl.ds(base + j, 8, stride=stride), :] = total[:8]
            slabs[pl.ds(base + j + used // 2, 8, stride=stride), :] = total[8:]

    copies_z, copies_x = [], []
    for part in range(2):
        project(att_z, r1zs.at[part], part * 2048, WZ)
        copies_z.append([
            send(r1zs.at[part, p], r1zr.at[part, k], sr1z, part * 7 + k, d) for k, (p, d) in enumerate(z_peers)
        ])
        project(att_x, r1xs.at[part], part * 2048 + WZ, WX)
        copies_x.append([
            send(r1xs.at[part, p], r1xr.at[part, k], sr1x, part * 7 + k, d) for k, (p, d) in enumerate(xy_peers)
        ])
    sums = []
    for part in range(2):
        for c in copies_x[part]:
            c.wait_recv()
        fold(r1xs.at[part], xy, r1xr.at[part], r2fx, part * 8 * PX, SX, PX)
        rows(r2xs, part, 8 * PX)[...] = rows(r2fx, part, 8 * PX)[...].astype(BF16)
        sums.append([
            send(rows(r2xs, part * 8 + p, PX), r2xr.at[part, k], sr2x, part * 7 + k, d)
            for k, (p, d) in enumerate(z_peers)
        ])
        for c in copies_z[part]:
            c.wait_recv()
        fold(r1zs.at[part], z, r1zr.at[part], r2fz, part * 8 * PZ, SZ, PZ)
        rows(r2zs, part, 8 * PZ)[...] = rows(r2fz, part, 8 * PZ)[...].astype(BF16)
        sums[part] += [
            send(rows(r2zs, part * 8 + p, PZ), r2zr.at[part, k], sr2z, part * 7 + k, d)
            for k, (p, d) in enumerate(xy_peers)
        ]
        pending += copies_x[part] + copies_z[part] + sums[part]

    squares = jnp.zeros((1, 1), F32)
    logits = [jnp.zeros((1, 1), F32)] * 4
    halves = []
    for part in range(2):
        for c in sums[part]:
            c.wait_recv()
        part_z = rows(r2fz, part * 8 + xy, PZ)[...]
        part_x = rows(r2fx, part * 8 + z, PX)[...]
        for k in range(7):
            part_z = part_z + r2zr[part, k].astype(F32)
            part_x = part_x + r2xr[part, k].astype(F32)
        for c in range(2):
            mine_rows = slice(c * 32 + part * 16, c * 32 + part * 16 + 16)
            piece = jnp.concatenate(
                [part_z[c * SZ // 2 : (c + 1) * SZ // 2], part_x[c * SX // 2 : (c + 1) * SX // 2]], axis=0
            )
            piece = hid[mine_rows] + piece
            hid[mine_rows] = piece
            gained = (piece * gain[mine_rows].astype(F32)).astype(BF16)
            g1s[part * 32 + c * 16 : part * 32 + c * 16 + 16] = gained
        halves.append([
            send(rows(g1s, part * 2 + p % 2, 16), rows(g1r, part * 16 + zc, 16), sg1, part * 15 + k, d)
            for k, (p, d) in enumerate(zc_peers)
        ])
        rows(g1r, part * 16 + zc, 16)[...] = rows(g1s, part * 2 + core, 16)[...]
        for c in range(2):
            mine_rows = slice(c * 32 + part * 16, c * 32 + part * 16 + 16)
            piece = hid[mine_rows]
            squares = squares + jnp.sum(piece * piece, keepdims=True)
            gained = g1s[part * 32 + c * 16 : part * 32 + c * 16 + 16].astype(F32)
            for e in range(4):
                weight = router[e * 64 + c * 32 + part * 16 : e * 64 + c * 32 + part * 16 + 16]
                logits[e] = logits[e] + jnp.sum(gained * weight, keepdims=True)
    spread = lax.rsqrt(squares * (1.0 / 8192) + 1e-05)
    logits = [v * spread for v in logits]

    first, second = ids_ref[0, 0], ids_ref[0, 1]
    zero = jnp.zeros((1, 1), F32)
    logit_a, logit_b = zero, zero
    for e in range(4):
        logit_a = logit_a + jnp.where(first == e, logits[e], zero)
        logit_b = logit_b + jnp.where(second == e, logits[e], zero)
    gate_a = 1.0 / (1.0 + jnp.exp(logit_b - logit_a))
    gate_b = 1.0 / (1.0 + jnp.exp(logit_a - logit_b))
    lane = iota((8, 128), 1)
    gates[...] = (
        jnp.where(lane == first, gate_a, 0.0) + jnp.where(lane == second, gate_b, 0.0)
        + jnp.where(lane == 4, spread, 0.0)
    )
    gate_copies = [
        send(gates.at[pl.ds(0, 1)], gate_in.at[zc, pl.ds(0, 1)], sgate, k, d)
        for k, (p, d) in enumerate(zc_peers)
    ]
    gate_in[zc] = gates[...]
    pending += halves[0] + halves[1] + gate_copies

    def block(part, j, i):
        if part == 0:
            return xa.at[core, (y + 4 - j) % 4, (x + 4 - i) % 4]
        return xb.at[core, (y + 4 - i) % 4, (x + 4 - j) % 4]

    def line(part, i):
        if part == 0:
            return xa.at[core, :, (x + 4 - i) % 4]
        return xb.at[core, (y + 4 - i) % 4]

    first_axis = [[d for _, d in y_peers], [d for _, d in x_peers]]
    second_axis = [[d for _, d in x_peers], [d for _, d in y_peers]]
    across = [[], []]
    middle = [{}, {}]
    onward = [{}, {}]

    def pass_on(part, j):
        ref = block(part, j, 0)
        for to, k in ((0, 0), (2, 4)):
            onward[part][k + j] = send(ref, ref, sg3, part * 12 + k + j, second_axis[part][to])
        if j == 2:
            onward[part][10] = send(ref, ref, sg3, part * 12 + 10, second_axis[part][1])
        if j == 2:
            across[part].append(send(line(part, 0), line(part, 0), sg4, part * 10, sibling))

    def relay(part, j):
        if j % 2 == 0:
            onward[part][j].wait_recv()
            ref, to = block(part, j, 1), second_axis[part][0]
        else:
            onward[part][4 + j].wait_recv()
            ref, to = block(part, j, 3), second_axis[part][2]
        onward[part][8 + j] = send(ref, ref, sg3, part * 12 + 8 + j, to)

    def begin(part):
        for c in halves[part]:
            c.wait_recv()
        g1f[...] = rows(g1r, part, 256)[...].astype(F32)
        ref = block(part, 0, 0)
        for j in range(16):
            ref[:, j * 128 : j * 128 + 128] = g1f[pl.ds(j, 16, stride=16), :].astype(BF16)
        for k in (1, 0, 2):
            middle[part][k] = send(ref, ref, sg2, part * 3 + k, first_axis[part][k])
        pass_on(part, 0)

    def come(part, j):
        middle[part][j - 1].wait_recv()
        pass_on(part, j)

    def lines(part):
        for j in (1, 2, 3):
            onward[part][j].wait_recv()
        across[part].append(send(line(part, 1), line(part, 1), sg4, part * 10 + 4, sibling))
        for j in (0, 2):
            onward[part][4 + j].wait_recv()
        across[part].append(send(line(part, 3), line(part, 3), sg4, part * 10 + 5, sibling))

    def last_line(part):
        for j in (0, 1, 3, 2):
            onward[part][8 + j].wait_recv()
        across[part].append(send(line(part, 2), line(part, 2), sg4, part * 10 + 6, sibling))

    begin(0)
    begin(1)
    for j in (1, 3):
        for part in range(2):
            come(part, j)
    for part in range(2):
        relay(part, 0)
    for part in range(2):
        come(part, 2)
    for j in (1, 3):
        for part in range(2):
            relay(part, j)
    lines(0)
    lines(1)
    for c in gate_copies:
        c.wait_recv()
    for i in range(16):
        gate_all[y, x, i : i + 1] = gate_in[i, 0:1]
    ref = gate_all.at[y, x]
    gate_middle = [send(ref, ref, sgate, 15 + k, d) for k, d in enumerate(first_axis[0])]
    last_line(0)
    last_line(1)
    for c in gate_middle:
        c.wait_recv()
    ref = gate_all.at[:, x]
    gate_onward = [send(ref, ref, sgate, 18 + k, d) for k, d in enumerate(second_axis[0])]
    loads[2].wait()
    loads[3].wait()
    acc[...] = jnp.zeros_like(acc)

    def into(half, part):
        rows_in = (xa, xb)[part][half].reshape(256, 2048)
        column = pl.ds(pl.multiple_of(half * 4096 + part * 2048, 2048), 2048)
        for k in range(2):
            acc[k] += nt(rows_in, w_in[k, :, column])

    into(core, 0)
    into(core, 1)
    for c in across[0]:
        c.wait_recv()
    into(1 - core, 0)
    for c in across[1]:
        c.wait_recv()
    into(1 - core, 1)
    pending += across[0] + across[1] + gate_middle + gate_onward
    for part in range(2):
        pending += list(middle[part].values()) + list(onward[part].values())

    loads[4].wait()
    for c in gate_onward:
        c.wait_recv()
    row_facts = gate_all[...].reshape(256, 128)
    lane = iota((256, 128), 1)
    gate = jnp.sum(jnp.where(lane == tier, row_facts, 0.0), axis=1, keepdims=True)
    factor = jnp.sum(jnp.where(lane == 4, row_facts, 0.0), axis=1, keepdims=True)
    gate_part = acc[0] * factor
    act[...] = (gate_part / (1.0 + jnp.exp(-gate_part)) * (acc[1] * factor)).astype(BF16)

    def down(half, part, t):
        column = pl.ds(pl.multiple_of(half * 4096 + part * 2048 + t * TN, TN), TN)
        return nn(act[...], w_down[:, column]) * gate

    chunks = range(4)

    def cut(t):
        return slice(t * TN, t * TN + TN)

    over = {}

    def sibling_chunk(t):
        for part in range(2):
            f0s[part, :, :, :, cut(t)] = down(1 - core, part, t).astype(BF16).reshape(4, 4, 16, TN)
            at = (part, slice(None), slice(None), slice(None), cut(t))
            over[part, t] = send(f0s.at[at], f0r.at[at], sf0, part * 4 + t, sibling)

    def toward(part, t, i):
        if part == 0:
            return f1s.at[0, :, (x + 4 + i) % 4, :, cut(t)]
        return f1s.at[1, (y + 4 + i) % 4, :, :, cut(t)]

    plain, opposite, joined, final = {}, {}, {}, {}

    def way(part, t):
        axis = second_axis[part]
        return (1, axis[0], axis[2]) if t % 2 == 0 else (-1, axis[2], axis[0])

    def own_chunk(t):
        for part in range(2):
            over[part, t].wait_recv()
            both = down(core, part, t) + f0r[part, :, :, :, cut(t)].reshape(256, TN).astype(F32)
            f1s[part, :, :, :, cut(t)] = both.astype(BF16).reshape(4, 4, 16, TN)
            step, ahead, behind = way(part, t)
            k = (part * 4 + t) * 3
            if t == 3:
                axis = second_axis[part]
                at = (part, slice(None), slice(None), cut(t))
                opposite[part, t] = send(toward(part, t, 2), fo.at[at], sf1, k, axis[1])
                plain[part, t] = send(toward(part, t, 1), fd.at[at], sf1, k + 1, axis[0])
                joined[part, t] = send(toward(part, t, 3), fcr.at[at], sf1, k + 2, axis[2])
                continue
            opposite[part, t] = send(toward(part, t, 2), fo.at[part, :, :, cut(t)], sf1, k, ahead)
            plain[part, t] = send(toward(part, t, -step), fd.at[part, :, :, cut(t)], sf1, k + 1, behind)

    def join_chunk(t):
        for part in range(2):
            step, ahead, behind = way(part, t)
            opposite[part, t].wait_recv()
            fcs[part, :, :, cut(t)] = (
                toward(part, t, step)[...].astype(F32) + fo[part, :, :, cut(t)].astype(F32)
            ).astype(BF16)
            at = (part, slice(None), slice(None), cut(t))
            joined[part, t] = send(fcs.at[at], fcr.at[at], sf1, (part * 4 + t) * 3 + 2, ahead)

    def end_chunk(t):
        for part in range(2):
            plain[part, t].wait_recv()
            joined[part, t].wait_recv()
            total = (
                toward(part, t, 0)[...].astype(F32)
                + fd[part, :, :, cut(t)].astype(F32)
                + fcr[part, :, :, cut(t)].astype(F32)
            )
            if t == 3:
                opposite[part, t].wait_recv()
                total = total + fo[part, :, :, cut(t)].astype(F32)
            f2s[part, :, :, cut(t)] = total.astype(BF16)
            for k, (p, d) in enumerate((y_peers, x_peers)[part]):
                final[part, t, k] = send(
                    f2s.at[part, p, :, cut(t)], f2r.at[part, k, :, cut(t)], sf2, (part * 4 + t) * 3 + k, d
                )

    last = {}

    def finish_chunk(t):
        half = t // 2
        for part in range(2):
            for k in range(3):
                final[part, t, k].wait_recv()
            for j in range(4):
                at = slice((t * 4 + j) * 128, (t * 4 + j + 1) * 128)
                total = f2s[part, (y, x)[part], :, at].astype(F32)
                for k in range(3):
                    total = total + f2r[part, k, :, at].astype(F32)
                f3f[pl.ds(half * 256 + part * 8 + t % 2 * 4 + j, 16, stride=16), :] = total
        if t % 2 == 1:
            rows(f3s, half, 256)[...] = rows(f3f, half, 256)[...].astype(BF16)
            for k, (p, d) in enumerate(zc_peers):
                last[half, k] = send(rows(f3s, half * 16 + p, 16), f3r.at[half, zc], sf3, half * 15 + k, d)
            f3r[half, zc] = rows(f3s, half * 16 + zc, 16)[...]

    sibling_chunk(0)
    sibling_chunk(1)
    own_chunk(0)
    sibling_chunk(2)
    own_chunk(1)
    sibling_chunk(3)
    own_chunk(2)
    join_chunk(0)
    own_chunk(3)
    join_chunk(1)
    join_chunk(2)
    end_chunk(0)
    end_chunk(1)
    end_chunk(2)
    finish_chunk(0)
    end_chunk(3)
    finish_chunk(1)
    finish_chunk(2)
    finish_chunk(3)
    for sent in (over, plain, opposite, joined, final, last):
        pending += list(sent.values())
    for c in pending:
        c.wait_send()
    for c in last.values():
        c.wait_recv()
    sums = []
    for c in range(2):
        parts = []
        for half in range(2):
            total = f3r[half, c].astype(F32)
            for k in range(1, 8):
                total = total + f3r[half, 2 * k + c].astype(F32)
            parts.append(total)
        sums += [parts[0][:8], parts[1][:8], parts[0][8:], parts[1][8:]]
    out_ref[...] = (hid[...] + jnp.concatenate(sums, axis=0)).astype(BF16)


def on_device(
    resid, query, fresh_kv, cache_home, kv_cache, cached_len, wo, norm_gain, w_router,
    expert_ids, w_gate, w_up, w_down,
):
    vmem, smem, hbm = (
        pl.BlockSpec(memory_space=pltpu.VMEM),
        pl.BlockSpec(memory_space=pltpu.SMEM),
        pl.BlockSpec(memory_space=pl.ANY),
    )
    v = pltpu.VMEM
    sem = lambda n: pltpu.SemaphoreType.DMA((2, n))
    out = pl.pallas_call(
        kernel,
        out_shape=jax.ShapeDtypeStruct((64, 128), BF16),
        in_specs=[vmem, smem, smem, vmem, vmem] + [hbm] * 8,
        out_specs=vmem,
        scratch_shapes=[
            v((128, 2048), BF16), v((128, 8192), BF16), v((2, 192, 8192), BF16), v((192, 8192), BF16),
            pltpu.SemaphoreType.DMA((8,)),
            v((1, 8192), BF16), v((64, 128), BF16), v((4, 8192), BF16),
            v((128, 128), BF16), v((128, 128), BF16), v((128, 128), F32), v((128, 128), BF16), v((128, 128), BF16),
            v((64, 128), F32), v((64, 128), F32), v((64, 128), F32), v((64, 128), F32),
            v((2, 8, 16, WZ), BF16), v((2, 7, 16, WZ), BF16), v((2, 8, 16, WX), BF16), v((2, 7, 16, WX), BF16),
            v((16 * PZ, 128), BF16), v((2, 7, PZ, 128), BF16), v((16 * PX, 128), BF16), v((2, 7, PX, 128), BF16),
            v((16 * PZ, 128), F32), v((16 * PX, 128), F32), v((64, 128), F32), v((256, 128), F32),
            v((64, 128), BF16), v((512, 128), BF16), v((256, 128), F32),
            v((8, 128), F32), v((16, 8, 128), F32), v((4, 4, 16, 128), F32),
            v((2, 4, 4, 16, 2048), BF16), v((2, 4, 4, 16, 2048), BF16),
            v((2, 256, 192), F32), v((256, 192), BF16),
            v((2, 4, 4, 16, 2048), BF16), v((2, 4, 4, 16, 2048), BF16), v((2, 4, 4, 16, 2048), BF16),
            v((2, 4, 16, 2048), BF16), v((2, 4, 16, 2048), BF16), v((2, 4, 16, 2048), BF16), v((2, 4, 16, 2048), BF16),
            v((2, 4, 16, 2048), BF16), v((2, 3, 16, 2048), BF16),
            v((512, 128), F32), v((512, 128), BF16), v((2, 16, 16, 128), BF16),
            sem(7), sem(7), sem(7), sem(7), sem(14), sem(14), sem(14), sem(14),
            sem(30), sem(21), sem(6), sem(24), sem(20), sem(8), sem(24), sem(24), sem(30),
        ],
        compiler_params=pltpu.CompilerParams(
            collective_id=0, has_side_effects=True, vmem_limit_bytes=60 * 2**20
        ),
    )(
        cache_home, cached_len, expert_ids, query, jnp.transpose(fresh_kv), resid,
        norm_gain.reshape(64, 128), jnp.transpose(w_router),
        kv_cache, wo, w_gate, w_up, w_down,
    )
    return out.reshape(1, 8192)


def solution(mesh):
    return jax.shard_map(
        on_device,
        mesh=mesh,
        in_specs=(
            P(("tier", "grp"), None),
            P("tier", "grp"),
            P("tier", "grp"),
            P("tier", None),
            P(("tier", "grp"), None, None),
            P(("tier", "grp")),
            P("grp", None),
            P(),
            P(),
            P(("tier", "grp"), None),
            P("tier", "grp", None),
            P("tier", "grp", None),
            P("tier", "grp", None),
        ),
        out_specs=P(("tier", "grp"), None),
        check_vma=False,
    )
```

```python
import functools
import math

import jax
import jax.numpy as jnp
from jax import lax
from jax.experimental import pallas as pl
from jax.experimental.pallas import tpu as pltpu
from jax.sharding import PartitionSpec as P

MESH = pl.DeviceIdType.MESH
F32 = jnp.float32
BF16 = jnp.bfloat16
WZ = 768
WX = 2048 - WZ
SZ, SX = 2 * WZ // 128, 2 * WX // 128
PZ, PX = -(-SZ // 16) * 16, -(-SX // 16) * 16
TN = 512


def iota(shape, dim):
    return lax.broadcasted_iota(jnp.int32, shape, dim)


def nt(a, b):
    return lax.dot_general(a, b, (((1,), (1,)), ((), ())), preferred_element_type=F32)


def nn(a, b):
    return jnp.dot(a, b, preferred_element_type=F32)


def kernel(
    home_ref, len_ref, ids_ref, query_ref, fresh_ref, resid_hbm, gain_hbm, router_hbm,
    cache_hbm, wo_hbm, gate_hbm, up_hbm, down_hbm,
    out_ref,
    cache, wo, w_in, w_down, local_sem,
    resid, gain, router_in, a1s, a1r, a1f, a2s, a2r, c1s, c1r, c2s, c2r,
    r1zs, r1zr, r1xs, r1xr, r2zs, r2zr, r2xs, r2xr,
    r2fz, r2fx, hid, router,
    g1s, g1r, g1f, gates, gate_in, gate_all, xa, xb, acc, act,
    f0s, f0r, f1s, fo, fd, fcs, fcr, f2s, f2r, f3f, f3s, f3r,
    sa1, sa2, sc1, sc2, sr1z, sr1x, sr2z, sr2x, sg1, sgate, sg2, sg3, sg4, sf0, sf1, sf2, sf3,
):
    tier, grp = lax.axis_index("tier"), lax.axis_index("grp")
    y_hi, core = tier // 2, tier % 2
    y_lo, z, x = grp // 32, (grp // 4) % 8, grp % 4
    y = y_hi * 2 + y_lo
    xy = y_lo * 4 + x
    zc = z * 2 + core

    def device(y, z, x, core):
        return ((y // 2) * 2 + core, (y % 2) * 32 + z * 4 + x)

    def send(src, dst, sems, k, to):
        copy = pltpu.make_async_remote_copy(
            src_ref=src, dst_ref=dst, send_sem=sems.at[0, k], recv_sem=sems.at[1, k],
            device_id=to, device_id_type=MESH,
        )
        copy.start()
        return copy

    far_first = (4, 3, 5, 2, 6, 1, 7)
    z_peers = [((z + k) % 8, device(y, (z + k) % 8, x, core)) for k in far_first]
    xy_peers = []
    for k_lo, k in ((1, 2), (0, 2), (1, 1), (1, 3), (0, 1), (0, 3), (1, 0)):
        px, p_lo = (x + k) % 4, (y_lo + k_lo) % 2
        xy_peers.append((p_lo * 4 + px, device(y_hi * 2 + p_lo, z, px, core)))
    zc_peers = []
    for k in far_first + (0,):
        for k_core in (1, 0)[: 2 if k else 1]:
            pz, pc = (z + k) % 8, (core + k_core) % 2
            zc_peers.append((pz * 2 + pc, device(y, pz, x, pc)))

    x_peers = [((x + k) % 4, device(y, z, (x + k) % 4, core)) for k in range(1, 4)]
    y_peers = [((y + k) % 4, device((y + k) % 4, z, x, core)) for k in range(1, 4)]
    sibling = device(y, z, x, 1 - core)
    far = [device(((1 - y_hi) * 2 + (y_lo + k) % 2), z, x, core) for k in range(2)]

    loads = [
        pltpu.make_async_copy(cache_hbm.at[0], cache, local_sem.at[0]),
        pltpu.make_async_copy(wo_hbm, wo, local_sem.at[1]),
        pltpu.make_async_copy(gate_hbm.at[0], w_in.at[0], local_sem.at[2]),
        pltpu.make_async_copy(up_hbm.at[0], w_in.at[1], local_sem.at[3]),
        pltpu.make_async_copy(down_hbm.at[0], w_down, local_sem.at[4]),
        pltpu.make_async_copy(resid_hbm, resid, local_sem.at[5]),
        pltpu.make_async_copy(gain_hbm, gain, local_sem.at[6]),
        pltpu.make_async_copy(router_hbm, router_in, local_sem.at[7]),
    ]
    barrier = pltpu.get_barrier_semaphore()
    greeted = [d for _, d in zc_peers] + [d for _, d in xy_peers] + far
    for d in greeted:
        pl.semaphore_signal(barrier, inc=1, device_id=d, device_id_type=MESH)

    slot = home_ref[...]
    place = ((slot >> 2) & 7) * 8 + (slot >> 5) * 4 + (slot & 3)
    to_slot = (iota((64, 64), 0) == place).astype(BF16)
    spread_fresh = (iota((32, 128), 1) == iota((32, 128), 0) + 32 * x).astype(BF16)
    by_slot_q = nn(to_slot, query_ref[...])
    by_slot_f = nn(nt(to_slot, fresh_ref[...]).astype(BF16), spread_fresh)
    for k in range(8):
        a1s[k * 16 : k * 16 + 16] = jnp.concatenate(
            [by_slot_q[k * 8 : k * 8 + 8], by_slot_f[k * 8 : k * 8 + 8]], axis=0
        ).astype(BF16)

    pl.semaphore_wait(barrier, len(greeted))

    def rows(ref, i, n):
        return ref.at[pl.ds(pl.multiple_of(i * n, n), n)]

    pending = []
    copies = [
        send(rows(a1s, p, 16), rows(a1r, z, 16), sa1, k, d) for k, (p, d) in enumerate(z_peers)
    ]
    rows(a1r, z, 16)[...] = rows(a1s, z, 16)[...]
    for load in loads[5:] + loads[:5]:
        load.start()
    r2fz[...] = jnp.zeros_like(r2fz)
    r2fx[...] = jnp.zeros_like(r2fx)
    for c in copies:
        c.wait_recv()
    pending += copies
    a1f[...] = a1r[...].astype(F32)
    for k in range(8):
        a2s[k * 16 : k * 16 + 16] = jnp.concatenate(
            [a1f[pl.ds(k, 8, stride=16), :], a1f[pl.ds(8 + k, 8, stride=16), :]], axis=0
        ).astype(BF16)
    copies = [
        send(rows(a2s, p, 16), rows(a2r, xy, 16), sa2, k, d) for k, (p, d) in enumerate(xy_peers)
    ]
    rows(a2r, xy, 16)[...] = rows(a2s, xy, 16)[...]
    for load in loads[5:]:
        load.wait()
    resid_row, router_rows = resid[...].astype(F32), router_in[...].astype(F32)
    for j in range(64):
        hid[j : j + 1] = resid_row[:, j * 128 : j * 128 + 128]
        router[pl.ds(j, 4, stride=64), :] = router_rows[:, j * 128 : j * 128 + 128]
    for c in copies:
        c.wait_recv()
    pending += copies

    head = iota((64, 128), 0)
    group = (head >> 5) * 4 + ((head & 7) >> 1)
    got = a2r[...].astype(F32).reshape(8, 16, 128)
    queries = got[:, :8].reshape(64, 128)
    news = got[:, 8:]
    new_key = (news[0] + news[1] + news[2] + news[3]).astype(BF16)
    new_value = (news[4] + news[5] + news[6] + news[7]).astype(BF16)
    of_group = (iota((64, 8), 1) == (iota((64, 8), 0) >> 5) * 4 + ((iota((64, 8), 0) & 7) >> 1)).astype(BF16)
    own_key = nn(of_group, new_key)
    own_value = nn(of_group, new_value)
    loads[0].wait()
    wide = jnp.concatenate(
        [jnp.where(group == j, queries, 0.0).astype(BF16) for j in range(8)], axis=1
    )
    scale = 1.0 / math.sqrt(128)
    scores = nt(wide, cache[:, :1024]) * scale
    scores = jnp.where(iota((64, 128), 1) < len_ref[0], scores, -1e30)
    own_score = jnp.sum(queries * own_key, axis=1, keepdims=True) * scale
    top = jnp.maximum(jnp.max(scores, axis=1, keepdims=True), own_score)
    weights = jnp.exp(scores - top)
    own_weight = jnp.exp(own_score - top)
    denominator = jnp.sum(weights, axis=1, keepdims=True) + own_weight
    weights = (weights / denominator).astype(BF16)
    own_weight = (own_weight / denominator).astype(BF16).astype(F32)
    mixed = nn(weights, cache[:, 1024:])
    outcome = own_weight * own_value
    for j in range(8):
        outcome = outcome + jnp.where(group == j, mixed[:, j * 128 : (j + 1) * 128], 0.0)
    c1s[...] = outcome.astype(BF16).astype(F32)

    copies = [
        send(rows(c1s, p, 8), rows(c1r, xy, 8), sc1, k, d) for k, (p, d) in enumerate(xy_peers)
    ]
    rows(c1r, xy, 8)[...] = rows(c1s, xy, 8)[...]
    for c in copies:
        c.wait_recv()
    pending += copies
    for k in range(8):
        c2s[k * 8 : k * 8 + 8] = c1r[pl.ds(k, 8, stride=8), :]
    copies = [
        send(rows(c2s, p, 8), rows(c2r, z, 8), sc2, k, d) for k, (p, d) in enumerate(z_peers)
    ]
    rows(c2r, z, 8)[...] = rows(c2s, z, 8)[...]
    for c in copies:
        c.wait_recv()
    pending += copies

    own = iota((64, 64), 1)
    own_z, own_xy = (own >> 2) & 7, (own >> 5) * 4 + (own & 3)
    by_head = c2r[...].astype(BF16)
    order_z = (iota((64, 64), 0) == own_z * 8 + own_xy).astype(BF16)
    order_x = (iota((64, 64), 0) == own_xy * 8 + own_z).astype(BF16)
    att_z = nn(nt(order_z, to_slot).astype(BF16), by_head).astype(BF16)
    att_x = nn(nt(order_x, to_slot).astype(BF16), by_head).astype(BF16)
    loads[1].wait()

    def project(att, ref, base, width):
        for at in range(0, width, width // 2):
            cut = slice(at, at + width // 2)
            lo = nn(att, wo[:, base + at : base + at + width // 2]).reshape(8, 8, width // 2)
            hi = nn(att, wo[:, 4096 + base + at : 4096 + base + at + width // 2]).reshape(8, 8, width // 2)
            ref[:, :, cut] = jnp.concatenate([lo, hi], axis=1).astype(BF16)

    def fold(sent, mine, received, slabs, base, used, stride):
        for j in range(used // 2):
            at = slice(j * 128, j * 128 + 128)
            total = sent[mine, :, at].astype(F32)
            for k in range(7):
                total = total + received[k, :, at].astype(F32)
            slabs[pl.ds(base + j, 8, stride=stride), :] = total[:8]
            slabs[pl.ds(base + j + used // 2, 8, stride=stride), :] = total[8:]

    copies_z, copies_x = [], []
    for part in range(2):
        project(att_z, r1zs.at[part], part * 2048, WZ)
        copies_z.append([
            send(r1zs.at[part, p], r1zr.at[part, k], sr1z, part * 7 + k, d) for k, (p, d) in enumerate(z_peers)
        ])
        project(att_x, r1xs.at[part], part * 2048 + WZ, WX)
        copies_x.append([
            send(r1xs.at[part, p], r1xr.at[part, k], sr1x, part * 7 + k, d) for k, (p, d) in enumerate(xy_peers)
        ])
    sums = []
    for part in range(2):
        for c in copies_x[part]:
            c.wait_recv()
        fold(r1xs.at[part], xy, r1xr.at[part], r2fx, part * 8 * PX, SX, PX)
        rows(r2xs, part, 8 * PX)[...] = rows(r2fx, part, 8 * PX)[...].astype(BF16)
        sums.append([
            send(rows(r2xs, part * 8 + p, PX), r2xr.at[part, k], sr2x, part * 7 + k, d)
            for k, (p, d) in enumerate(z_peers)
        ])
        for c in copies_z[part]:
            c.wait_recv()
        fold(r1zs.at[part], z, r1zr.at[part], r2fz, part * 8 * PZ, SZ, PZ)
        rows(r2zs, part, 8 * PZ)[...] = rows(r2fz, part, 8 * PZ)[...].astype(BF16)
        sums[part] += [
            send(rows(r2zs, part * 8 + p, PZ), r2zr.at[part, k], sr2z, part * 7 + k, d)
            for k, (p, d) in enumerate(xy_peers)
        ]
        pending += copies_x[part] + copies_z[part] + sums[part]

    squares = jnp.zeros((1, 1), F32)
    logits = [jnp.zeros((1, 1), F32)] * 4
    halves = []
    for part in range(2):
        for c in sums[part]:
            c.wait_recv()
        part_z = rows(r2fz, part * 8 + xy, PZ)[...]
        part_x = rows(r2fx, part * 8 + z, PX)[...]
        for k in range(7):
            part_z = part_z + r2zr[part, k].astype(F32)
            part_x = part_x + r2xr[part, k].astype(F32)
        for c in range(2):
            mine_rows = slice(c * 32 + part * 16, c * 32 + part * 16 + 16)
            piece = jnp.concatenate(
                [part_z[c * SZ // 2 : (c + 1) * SZ // 2], part_x[c * SX // 2 : (c + 1) * SX // 2]], axis=0
            )
            piece = hid[mine_rows] + piece
            hid[mine_rows] = piece
            gained = (piece * gain[mine_rows].astype(F32)).astype(BF16)
            g1s[part * 32 + c * 16 : part * 32 + c * 16 + 16] = gained
        halves.append([
            send(rows(g1s, part * 2 + p % 2, 16), rows(g1r, part * 16 + zc, 16), sg1, part * 15 + k, d)
            for k, (p, d) in enumerate(zc_peers)
        ])
        rows(g1r, part * 16 + zc, 16)[...] = rows(g1s, part * 2 + core, 16)[...]
        for c in range(2):
            mine_rows = slice(c * 32 + part * 16, c * 32 + part * 16 + 16)
            piece = hid[mine_rows]
            squares = squares + jnp.sum(piece * piece, keepdims=True)
            gained = g1s[part * 32 + c * 16 : part * 32 + c * 16 + 16].astype(F32)
            for e in range(4):
                weight = router[e * 64 + c * 32 + part * 16 : e * 64 + c * 32 + part * 16 + 16]
                logits[e] = logits[e] + jnp.sum(gained * weight, keepdims=True)
    spread = lax.rsqrt(squares * (1.0 / 8192) + 1e-05)
    logits = [v * spread for v in logits]

    first, second = ids_ref[0, 0], ids_ref[0, 1]
    zero = jnp.zeros((1, 1), F32)
    logit_a, logit_b = zero, zero
    for e in range(4):
        logit_a = logit_a + jnp.where(first == e, logits[e], zero)
        logit_b = logit_b + jnp.where(second == e, logits[e], zero)
    gate_a = 1.0 / (1.0 + jnp.exp(logit_b - logit_a))
    gate_b = 1.0 / (1.0 + jnp.exp(logit_a - logit_b))
    lane = iota((8, 128), 1)
    gates[...] = (
        jnp.where(lane == first, gate_a, 0.0) + jnp.where(lane == second, gate_b, 0.0)
        + jnp.where(lane == 4, spread, 0.0)
    )
    gate_copies = [
        send(gates.at[pl.ds(0, 1)], gate_in.at[zc, pl.ds(0, 1)], sgate, k, d)
        for k, (p, d) in enumerate(zc_peers)
    ]
    gate_in[zc] = gates[...]
    pending += halves[0] + halves[1] + gate_copies

    def block(part, j, i):
        if part == 0:
            return xa.at[core, (y + 4 - j) % 4, (x + 4 - i) % 4]
        return xb.at[core, (y + 4 - i) % 4, (x + 4 - j) % 4]

    def line(part, i):
        if part == 0:
            return xa.at[core, :, (x + 4 - i) % 4]
        return xb.at[core, (y + 4 - i) % 4]

    first_axis = [[d for _, d in y_peers], [d for _, d in x_peers]]
    second_axis = [[d for _, d in x_peers], [d for _, d in y_peers]]
    across = [[], []]
    middle = [{}, {}]
    onward = [{}, {}]

    def pass_on(part, j):
        ref = block(part, j, 0)
        for to, k in ((0, 0), (2, 4)):
            onward[part][k + j] = send(ref, ref, sg3, part * 12 + k + j, second_axis[part][to])
        if j == 2:
            onward[part][10] = send(ref, ref, sg3, part * 12 + 10, second_axis[part][1])
        if j == 2:
            across[part].append(send(line(part, 0), line(part, 0), sg4, part * 10, sibling))

    def relay(part, j):
        if j % 2 == 0:
            onward[part][j].wait_recv()
            ref, to = block(part, j, 1), second_axis[part][0]
        else:
            onward[part][4 + j].wait_recv()
            ref, to = block(part, j, 3), second_axis[part][2]
        onward[part][8 + j] = send(ref, ref, sg3, part * 12 + 8 + j, to)

    def begin(part):
        for c in halves[part]:
            c.wait_recv()
        g1f[...] = rows(g1r, part, 256)[...].astype(F32)
        ref = block(part, 0, 0)
        for j in range(16):
            ref[:, j * 128 : j * 128 + 128] = g1f[pl.ds(j, 16, stride=16), :].astype(BF16)
        for k in (1, 0, 2):
            middle[part][k] = send(ref, ref, sg2, part * 3 + k, first_axis[part][k])
        pass_on(part, 0)

    def come(part, j):
        middle[part][j - 1].wait_recv()
        pass_on(part, j)

    def lines(part):
        for j in (1, 2, 3):
            onward[part][j].wait_recv()
        across[part].append(send(line(part, 1), line(part, 1), sg4, part * 10 + 4, sibling))
        for j in (0, 2):
            onward[part][4 + j].wait_recv()
        across[part].append(send(line(part, 3), line(part, 3), sg4, part * 10 + 5, sibling))

    def last_line(part):
        for j in (0, 1, 3, 2):
            onward[part][8 + j].wait_recv()
        across[part].append(send(line(part, 2), line(part, 2), sg4, part * 10 + 6, sibling))

    begin(0)
    begin(1)
    for j in (1, 3):
        for part in range(2):
            come(part, j)
    for part in range(2):
        relay(part, 0)
    for part in range(2):
        come(part, 2)
    for j in (1, 3):
        for part in range(2):
            relay(part, j)
    lines(0)
    lines(1)
    for c in gate_copies:
        c.wait_recv()
    for i in range(16):
        gate_all[y, x, i : i + 1] = gate_in[i, 0:1]
    ref = gate_all.at[y, x]
    gate_middle = [send(ref, ref, sgate, 15 + k, d) for k, d in enumerate(first_axis[0])]
    last_line(0)
    last_line(1)
    for c in gate_middle:
        c.wait_recv()
    ref = gate_all.at[:, x]
    gate_onward = [send(ref, ref, sgate, 18 + k, d) for k, d in enumerate(second_axis[0])]
    loads[2].wait()
    loads[3].wait()

    def into(half, part, first=False):
        rows_in = (xa, xb)[part][half].reshape(256, 2048)
        column = pl.ds(pl.multiple_of(half * 4096 + part * 2048, 2048), 2048)
        for k in range(2):
            product = nt(rows_in, w_in[k, :, column])
            acc[k] = product if first else acc[k] + product

    into(core, 0, first=True)
    into(core, 1)
    for c in across[0]:
        c.wait_recv()
    into(1 - core, 0)
    for c in across[1]:
        c.wait_recv()
    into(1 - core, 1)
    pending += across[0] + across[1] + gate_middle + gate_onward
    for part in range(2):
        pending += list(middle[part].values()) + list(onward[part].values())

    loads[4].wait()
    for c in gate_onward:
        c.wait_recv()
    row_facts = gate_all[...].reshape(256, 128)
    lane = iota((256, 128), 1)
    gate = jnp.sum(jnp.where(lane == tier, row_facts, 0.0), axis=1, keepdims=True)
    factor = jnp.sum(jnp.where(lane == 4, row_facts, 0.0), axis=1, keepdims=True)
    gate_part = acc[0] * factor
    act[...] = (gate_part / (1.0 + jnp.exp(-gate_part)) * (acc[1] * factor)).astype(BF16)

    def down(half, part, t):
        column = pl.ds(pl.multiple_of(half * 4096 + part * 2048 + t * TN, TN), TN)
        return nn(act[...], w_down[:, column]) * gate

    chunks = range(4)

    def cut(t):
        return slice(t * TN, t * TN + TN)

    over = {}

    def sibling_chunk(t):
        for part in range(2):
            f0s[part, :, :, :, cut(t)] = down(1 - core, part, t).astype(BF16).reshape(4, 4, 16, TN)
            at = (part, slice(None), slice(None), slice(None), cut(t))
            over[part, t] = send(f0s.at[at], f0r.at[at], sf0, part * 4 + t, sibling)

    def toward(part, t, i):
        if part == 0:
            return f1s.at[0, :, (x + 4 + i) % 4, :, cut(t)]
        return f1s.at[1, (y + 4 + i) % 4, :, :, cut(t)]

    plain, opposite, joined, final = {}, {}, {}, {}

    def way(part, t):
        axis = second_axis[part]
        return (1, axis[0], axis[2]) if t % 2 == 0 else (-1, axis[2], axis[0])

    def own_chunk(t):
        for part in range(2):
            over[part, t].wait_recv()
            both = down(core, part, t) + f0r[part, :, :, :, cut(t)].reshape(256, TN).astype(F32)
            f1s[part, :, :, :, cut(t)] = both.astype(BF16).reshape(4, 4, 16, TN)
            step, ahead, behind = way(part, t)
            k = (part * 4 + t) * 3
            if t == 3:
                axis = second_axis[part]
                at = (part, slice(None), slice(None), cut(t))
                opposite[part, t] = send(toward(part, t, 2), fo.at[at], sf1, k, axis[1])
                plain[part, t] = send(toward(part, t, 1), fd.at[at], sf1, k + 1, axis[0])
                joined[part, t] = send(toward(part, t, 3), fcr.at[at], sf1, k + 2, axis[2])
                continue
            opposite[part, t] = send(toward(part, t, 2), fo.at[part, :, :, cut(t)], sf1, k, ahead)
            plain[part, t] = send(toward(part, t, -step), fd.at[part, :, :, cut(t)], sf1, k + 1, behind)

    def join_chunk(t):
        for part in range(2):
            step, ahead, behind = way(part, t)
            opposite[part, t].wait_recv()
            fcs[part, :, :, cut(t)] = (
                toward(part, t, step)[...].astype(F32) + fo[part, :, :, cut(t)].astype(F32)
            ).astype(BF16)
            at = (part, slice(None), slice(None), cut(t))
            joined[part, t] = send(fcs.at[at], fcr.at[at], sf1, (part * 4 + t) * 3 + 2, ahead)

    def end_chunk(t):
        for part in range(2):
            plain[part, t].wait_recv()
            joined[part, t].wait_recv()
            total = (
                toward(part, t, 0)[...].astype(F32)
                + fd[part, :, :, cut(t)].astype(F32)
                + fcr[part, :, :, cut(t)].astype(F32)
            )
            if t == 3:
                opposite[part, t].wait_recv()
                total = total + fo[part, :, :, cut(t)].astype(F32)
            f2s[part, :, :, cut(t)] = total.astype(BF16)
            for k, (p, d) in enumerate((y_peers, x_peers)[part]):
                final[part, t, k] = send(
                    f2s.at[part, p, :, cut(t)], f2r.at[part, k, :, cut(t)], sf2, (part * 4 + t) * 3 + k, d
                )

    last = {}

    def finish_chunk(t):
        half = t // 2
        for part in range(2):
            for k in range(3):
                final[part, t, k].wait_recv()
            for j in range(4):
                at = slice((t * 4 + j) * 128, (t * 4 + j + 1) * 128)
                total = f2s[part, (y, x)[part], :, at].astype(F32)
                for k in range(3):
                    total = total + f2r[part, k, :, at].astype(F32)
                f3f[pl.ds(half * 256 + part * 8 + t % 2 * 4 + j, 16, stride=16), :] = total
        if t % 2 == 1:
            rows(f3s, half, 256)[...] = rows(f3f, half, 256)[...].astype(BF16)
            for k, (p, d) in enumerate(zc_peers):
                last[half, k] = send(rows(f3s, half * 16 + p, 16), f3r.at[half, zc], sf3, half * 15 + k, d)
            f3r[half, zc] = rows(f3s, half * 16 + zc, 16)[...]

    sibling_chunk(0)
    sibling_chunk(1)
    own_chunk(0)
    sibling_chunk(2)
    own_chunk(1)
    sibling_chunk(3)
    own_chunk(2)
    join_chunk(0)
    own_chunk(3)
    join_chunk(1)
    join_chunk(2)
    end_chunk(0)
    end_chunk(1)
    end_chunk(2)
    finish_chunk(0)
    end_chunk(3)
    finish_chunk(1)
    finish_chunk(2)
    finish_chunk(3)
    for sent in (over, plain, opposite, joined, final, last):
        pending += list(sent.values())
    for c in pending:
        c.wait_send()
    for c in last.values():
        c.wait_recv()
    sums = []
    for c in range(2):
        parts = []
        for half in range(2):
            total = f3r[half, c].astype(F32)
            for k in range(1, 8):
                total = total + f3r[half, 2 * k + c].astype(F32)
            parts.append(total)
        sums += [parts[0][:8], parts[1][:8], parts[0][8:], parts[1][8:]]
    out_ref[...] = (hid[...] + jnp.concatenate(sums, axis=0)).astype(BF16)


def on_device(
    resid, query, fresh_kv, cache_home, kv_cache, cached_len, wo, norm_gain, w_router,
    expert_ids, w_gate, w_up, w_down,
):
    vmem, smem, hbm = (
        pl.BlockSpec(memory_space=pltpu.VMEM),
        pl.BlockSpec(memory_space=pltpu.SMEM),
        pl.BlockSpec(memory_space=pl.ANY),
    )
    v = pltpu.VMEM
    sem = lambda n: pltpu.SemaphoreType.DMA((2, n))
    out = pl.pallas_call(
        kernel,
        out_shape=jax.ShapeDtypeStruct((64, 128), BF16),
        in_specs=[vmem, smem, smem, vmem, vmem] + [hbm] * 8,
        out_specs=vmem,
        scratch_shapes=[
            v((128, 2048), BF16), v((128, 8192), BF16), v((2, 192, 8192), BF16), v((192, 8192), BF16),
            pltpu.SemaphoreType.DMA((8,)),
            v((1, 8192), BF16), v((64, 128), BF16), v((4, 8192), BF16),
            v((128, 128), BF16), v((128, 128), BF16), v((128, 128), F32), v((128, 128), BF16), v((128, 128), BF16),
            v((64, 128), F32), v((64, 128), F32), v((64, 128), F32), v((64, 128), F32),
            v((2, 8, 16, WZ), BF16), v((2, 7, 16, WZ), BF16), v((2, 8, 16, WX), BF16), v((2, 7, 16, WX), BF16),
            v((16 * PZ, 128), BF16), v((2, 7, PZ, 128), BF16), v((16 * PX, 128), BF16), v((2, 7, PX, 128), BF16),
            v((16 * PZ, 128), F32), v((16 * PX, 128), F32), v((64, 128), F32), v((512, 128), F32),
            v((64, 128), BF16), v((512, 128), BF16), v((256, 128), F32),
            v((8, 128), F32), v((16, 8, 128), F32), v((4, 4, 16, 128), F32),
            v((2, 4, 4, 16, 2048), BF16), v((2, 4, 4, 16, 2048), BF16),
            v((2, 256, 192), F32), v((256, 192), BF16),
            v((2, 4, 4, 16, 2048), BF16), v((2, 4, 4, 16, 2048), BF16), v((2, 4, 4, 16, 2048), BF16),
            v((2, 4, 16, 2048), BF16), v((2, 4, 16, 2048), BF16), v((2, 4, 16, 2048), BF16), v((2, 4, 16, 2048), BF16),
            v((2, 4, 16, 2048), BF16), v((2, 3, 16, 2048), BF16),
            v((512, 128), F32), v((512, 128), BF16), v((2, 16, 16, 128), BF16),
            sem(7), sem(7), sem(7), sem(7), sem(14), sem(14), sem(14), sem(14),
            sem(30), sem(21), sem(6), sem(24), sem(20), sem(8), sem(24), sem(24), sem(30),
        ],
        compiler_params=pltpu.CompilerParams(
            collective_id=0, has_side_effects=True, vmem_limit_bytes=60 * 2**20
        ),
    )(
        cache_home, cached_len, expert_ids, query, jnp.transpose(fresh_kv), resid,
        norm_gain.reshape(64, 128), jnp.transpose(w_router),
        kv_cache, wo, w_gate, w_up, w_down,
    )
    return out.reshape(1, 8192)


def solution(mesh):
    return jax.shard_map(
        on_device,
        mesh=mesh,
        in_specs=(
            P(("tier", "grp"), None),
            P("tier", "grp"),
            P("tier", "grp"),
            P("tier", None),
            P(("tier", "grp"), None, None),
            P(("tier", "grp")),
            P("grp", None),
            P(),
            P(),
            P(("tier", "grp"), None),
            P("tier", "grp", None),
            P("tier", "grp", None),
            P("tier", "grp", None),
        ),
        out_specs=P(("tier", "grp"), None),
        check_vma=False,
    )
```

```python
import functools
import math

import jax
import jax.numpy as jnp
from jax import lax
from jax.experimental import pallas as pl
from jax.experimental.pallas import tpu as pltpu
from jax.sharding import PartitionSpec as P

MESH = pl.DeviceIdType.MESH
F32 = jnp.float32
BF16 = jnp.bfloat16
WZ = 768
WX = 2048 - WZ
SZ, SX = 2 * WZ // 128, 2 * WX // 128
PZ, PX = -(-SZ // 16) * 16, -(-SX // 16) * 16
TN = 512


def iota(shape, dim):
    return lax.broadcasted_iota(jnp.int32, shape, dim)


def nt(a, b):
    return lax.dot_general(a, b, (((1,), (1,)), ((), ())), preferred_element_type=F32)


def nn(a, b):
    return jnp.dot(a, b, preferred_element_type=F32)


def kernel(
    home_ref, len_ref, ids_ref, query_ref, fresh_ref, resid_hbm, gain_hbm, router_hbm,
    cache_hbm, wo_hbm, gate_hbm, up_hbm, down_hbm,
    out_ref,
    cache, wo, w_in, w_down, local_sem,
    resid, gain, router_in, a1s, a1r, a1f, a2s, a2r, c1s, c1r, c2s, c2r,
    r1zs, r1zr, r1xs, r1xr, r2zs, r2zr, r2xs, r2xr,
    r2fz, r2fx, hid, router,
    g1s, g1r, g1f, gates, gate_in, gate_all, xa, xb, acc, act,
    f0s, f0r, f1s, fo, fd, fcs, fcr, f2s, f2r, f3f, f3s, f3r,
    sa1, sa2, sc1, sc2, sr1z, sr1x, sr2z, sr2x, sg1, sgate, sg2, sg3, sg4, sf0, sf1, sf2, sf3,
):
    tier, grp = lax.axis_index("tier"), lax.axis_index("grp")
    y_hi, core = tier // 2, tier % 2
    y_lo, z, x = grp // 32, (grp // 4) % 8, grp % 4
    y = y_hi * 2 + y_lo
    xy = y_lo * 4 + x
    zc = z * 2 + core

    def device(y, z, x, core):
        return ((y // 2) * 2 + core, (y % 2) * 32 + z * 4 + x)

    def send(src, dst, sems, k, to):
        copy = pltpu.make_async_remote_copy(
            src_ref=src, dst_ref=dst, send_sem=sems.at[0, k], recv_sem=sems.at[1, k],
            device_id=to, device_id_type=MESH,
        )
        copy.start()
        return copy

    far_first = (4, 3, 5, 2, 6, 1, 7)
    z_peers = [((z + k) % 8, device(y, (z + k) % 8, x, core)) for k in far_first]
    xy_peers = []
    for k_lo, k in ((1, 2), (0, 2), (1, 1), (1, 3), (0, 1), (0, 3), (1, 0)):
        px, p_lo = (x + k) % 4, (y_lo + k_lo) % 2
        xy_peers.append((p_lo * 4 + px, device(y_hi * 2 + p_lo, z, px, core)))
    zc_peers = []
    for k in far_first + (0,):
        for k_core in (1, 0)[: 2 if k else 1]:
            pz, pc = (z + k) % 8, (core + k_core) % 2
            zc_peers.append((pz * 2 + pc, device(y, pz, x, pc)))

    x_peers = [((x + k) % 4, device(y, z, (x + k) % 4, core)) for k in range(1, 4)]
    y_peers = [((y + k) % 4, device((y + k) % 4, z, x, core)) for k in range(1, 4)]
    sibling = device(y, z, x, 1 - core)
    far = [device(((1 - y_hi) * 2 + (y_lo + k) % 2), z, x, core) for k in range(2)]

    loads = [
        pltpu.make_async_copy(cache_hbm.at[0], cache, local_sem.at[0]),
        pltpu.make_async_copy(wo_hbm, wo, local_sem.at[1]),
        pltpu.make_async_copy(gate_hbm.at[0], w_in.at[0], local_sem.at[2]),
        pltpu.make_async_copy(up_hbm.at[0], w_in.at[1], local_sem.at[3]),
        pltpu.make_async_copy(down_hbm.at[0], w_down, local_sem.at[4]),
        pltpu.make_async_copy(resid_hbm, resid, local_sem.at[5]),
        pltpu.make_async_copy(gain_hbm, gain, local_sem.at[6]),
        pltpu.make_async_copy(router_hbm, router_in, local_sem.at[7]),
    ]
    barrier = pltpu.get_barrier_semaphore()
    greeted = [d for _, d in zc_peers] + [d for _, d in xy_peers] + far
    for d in greeted:
        pl.semaphore_signal(barrier, inc=1, device_id=d, device_id_type=MESH)

    slot = home_ref[...]
    place = ((slot >> 2) & 7) * 8 + (slot >> 5) * 4 + (slot & 3)
    to_slot = (iota((64, 64), 0) == place).astype(BF16)
    spread_fresh = (iota((32, 128), 1) == iota((32, 128), 0) + 32 * x).astype(BF16)
    by_slot_q = nn(to_slot, query_ref[...])
    by_slot_f = nn(nt(to_slot, fresh_ref[...]).astype(BF16), spread_fresh)
    for k in range(8):
        a1s[k * 16 : k * 16 + 16] = jnp.concatenate(
            [by_slot_q[k * 8 : k * 8 + 8], by_slot_f[k * 8 : k * 8 + 8]], axis=0
        ).astype(BF16)

    pl.semaphore_wait(barrier, len(greeted))

    def rows(ref, i, n):
        return ref.at[pl.ds(pl.multiple_of(i * n, n), n)]

    pending = []
    copies = [
        send(rows(a1s, p, 16), rows(a1r, z, 16), sa1, k, d) for k, (p, d) in enumerate(z_peers)
    ]
    rows(a1r, z, 16)[...] = rows(a1s, z, 16)[...]
    for load in loads[5:] + loads[:5]:
        load.start()
    r2fz[...] = jnp.zeros_like(r2fz)
    r2fx[...] = jnp.zeros_like(r2fx)
    for c in copies:
        c.wait_recv()
    pending += copies
    a1f[...] = a1r[...].astype(F32)
    for k in range(8):
        a2s[k * 16 : k * 16 + 16] = jnp.concatenate(
            [a1f[pl.ds(k, 8, stride=16), :], a1f[pl.ds(8 + k, 8, stride=16), :]], axis=0
        ).astype(BF16)
    copies = [
        send(rows(a2s, p, 16), rows(a2r, xy, 16), sa2, k, d) for k, (p, d) in enumerate(xy_peers)
    ]
    rows(a2r, xy, 16)[...] = rows(a2s, xy, 16)[...]
    for load in loads[5:]:
        load.wait()
    resid_row, router_rows = resid[...].astype(F32), router_in[...].astype(F32)
    for j in range(64):
        hid[j : j + 1] = resid_row[:, j * 128 : j * 128 + 128]
        router[pl.ds(j, 4, stride=64), :] = router_rows[:, j * 128 : j * 128 + 128]
    for c in copies:
        c.wait_recv()
    pending += copies

    head = iota((64, 128), 0)
    group = (head >> 5) * 4 + ((head & 7) >> 1)
    got = a2r[...].astype(F32).reshape(8, 16, 128)
    queries = got[:, :8].reshape(64, 128)
    news = got[:, 8:]
    new_key = (news[0] + news[1] + news[2] + news[3]).astype(BF16)
    new_value = (news[4] + news[5] + news[6] + news[7]).astype(BF16)
    of_group = (iota((64, 8), 1) == (iota((64, 8), 0) >> 5) * 4 + ((iota((64, 8), 0) & 7) >> 1)).astype(BF16)
    own_key = nn(of_group, new_key)
    own_value = nn(of_group, new_value)
    loads[0].wait()
    wide = jnp.concatenate(
        [jnp.where(group == j, queries, 0.0).astype(BF16) for j in range(8)], axis=1
    )
    scale = 1.0 / math.sqrt(128)
    scores = nt(wide, cache[:, :1024]) * scale
    scores = jnp.where(iota((64, 128), 1) < len_ref[0], scores, -1e30)
    own_score = jnp.sum(queries * own_key, axis=1, keepdims=True) * scale
    top = jnp.maximum(jnp.max(scores, axis=1, keepdims=True), own_score)
    weights = jnp.exp(scores - top)
    own_weight = jnp.exp(own_score - top)
    denominator = jnp.sum(weights, axis=1, keepdims=True) + own_weight
    weights = (weights / denominator).astype(BF16)
    own_weight = (own_weight / denominator).astype(BF16).astype(F32)
    mixed = nn(weights, cache[:, 1024:])
    outcome = own_weight * own_value
    for j in range(8):
        outcome = outcome + jnp.where(group == j, mixed[:, j * 128 : (j + 1) * 128], 0.0)
    c1s[...] = outcome.astype(BF16).astype(F32)

    copies = [
        send(rows(c1s, p, 8), rows(c1r, xy, 8), sc1, k, d) for k, (p, d) in enumerate(xy_peers)
    ]
    rows(c1r, xy, 8)[...] = rows(c1s, xy, 8)[...]
    for c in copies:
        c.wait_recv()
    pending += copies
    for k in range(8):
        c2s[k * 8 : k * 8 + 8] = c1r[pl.ds(k, 8, stride=8), :]
    copies = [
        send(rows(c2s, p, 8), rows(c2r, z, 8), sc2, k, d) for k, (p, d) in enumerate(z_peers)
    ]
    rows(c2r, z, 8)[...] = rows(c2s, z, 8)[...]
    for c in copies:
        c.wait_recv()
    pending += copies

    own = iota((64, 64), 1)
    own_z, own_xy = (own >> 2) & 7, (own >> 5) * 4 + (own & 3)
    by_head = c2r[...].astype(BF16)
    order_z = (iota((64, 64), 0) == own_z * 8 + own_xy).astype(BF16)
    order_x = (iota((64, 64), 0) == own_xy * 8 + own_z).astype(BF16)
    att_z = nn(nt(order_z, to_slot).astype(BF16), by_head).astype(BF16)
    att_x = nn(nt(order_x, to_slot).astype(BF16), by_head).astype(BF16)
    loads[1].wait()

    def project(att, ref, base, width):
        for at in range(0, width, width // 2):
            cut = slice(at, at + width // 2)
            lo = nn(att, wo[:, base + at : base + at + width // 2]).reshape(8, 8, width // 2)
            hi = nn(att, wo[:, 4096 + base + at : 4096 + base + at + width // 2]).reshape(8, 8, width // 2)
            ref[:, :, cut] = jnp.concatenate([lo, hi], axis=1).astype(BF16)

    def fold(sent, mine, received, slabs, base, used, stride):
        for j in range(used // 2):
            at = slice(j * 128, j * 128 + 128)
            total = sent[mine, :, at].astype(F32)
            for k in range(7):
                total = total + received[k, :, at].astype(F32)
            slabs[pl.ds(base + j, 8, stride=stride), :] = total[:8]
            slabs[pl.ds(base + j + used // 2, 8, stride=stride), :] = total[8:]

    copies_z, copies_x = [], []
    for part in range(2):
        project(att_z, r1zs.at[part], part * 2048, WZ)
        copies_z.append([
            send(r1zs.at[part, p], r1zr.at[part, k], sr1z, part * 7 + k, d) for k, (p, d) in enumerate(z_peers)
        ])
        project(att_x, r1xs.at[part], part * 2048 + WZ, WX)
        copies_x.append([
            send(r1xs.at[part, p], r1xr.at[part, k], sr1x, part * 7 + k, d) for k, (p, d) in enumerate(xy_peers)
        ])
    sums = []
    for part in range(2):
        for c in copies_x[part]:
            c.wait_recv()
        fold(r1xs.at[part], xy, r1xr.at[part], r2fx, part * 8 * PX, SX, PX)
        rows(r2xs, part, 8 * PX)[...] = rows(r2fx, part, 8 * PX)[...].astype(BF16)
        sums.append([
            send(rows(r2xs, part * 8 + p, PX), r2xr.at[part, k], sr2x, part * 7 + k, d)
            for k, (p, d) in enumerate(z_peers)
        ])
        for c in copies_z[part]:
            c.wait_recv()
        fold(r1zs.at[part], z, r1zr.at[part], r2fz, part * 8 * PZ, SZ, PZ)
        rows(r2zs, part, 8 * PZ)[...] = rows(r2fz, part, 8 * PZ)[...].astype(BF16)
        sums[part] += [
            send(rows(r2zs, part * 8 + p, PZ), r2zr.at[part, k], sr2z, part * 7 + k, d)
            for k, (p, d) in enumerate(xy_peers)
        ]
        pending += copies_x[part] + copies_z[part] + sums[part]

    squares = jnp.zeros((1, 1), F32)
    logits = [jnp.zeros((1, 1), F32)] * 4
    halves = []
    for part in range(2):
        for c in sums[part]:
            c.wait_recv()
        part_z = rows(r2fz, part * 8 + xy, PZ)[...]
        part_x = rows(r2fx, part * 8 + z, PX)[...]
        for k in range(7):
            part_z = part_z + r2zr[part, k].astype(F32)
            part_x = part_x + r2xr[part, k].astype(F32)
        for c in range(2):
            mine_rows = slice(c * 32 + part * 16, c * 32 + part * 16 + 16)
            piece = jnp.concatenate(
                [part_z[c * SZ // 2 : (c + 1) * SZ // 2], part_x[c * SX // 2 : (c + 1) * SX // 2]], axis=0
            )
            piece = hid[mine_rows] + piece
            hid[mine_rows] = piece
            gained = (piece * gain[mine_rows].astype(F32)).astype(BF16)
            g1s[part * 32 + c * 16 : part * 32 + c * 16 + 16] = gained
        halves.append([
            send(rows(g1s, part * 2 + p % 2, 16), rows(g1r, part * 16 + zc, 16), sg1, part * 15 + k, d)
            for k, (p, d) in enumerate(zc_peers)
        ])
        rows(g1r, part * 16 + zc, 16)[...] = rows(g1s, part * 2 + core, 16)[...]
        for c in range(2):
            mine_rows = slice(c * 32 + part * 16, c * 32 + part * 16 + 16)
            piece = hid[mine_rows]
            squares = squares + jnp.sum(piece * piece, keepdims=True)
            gained = g1s[part * 32 + c * 16 : part * 32 + c * 16 + 16].astype(F32)
            for e in range(4):
                weight = router[e * 64 + c * 32 + part * 16 : e * 64 + c * 32 + part * 16 + 16]
                logits[e] = logits[e] + jnp.sum(gained * weight, keepdims=True)
    spread = lax.rsqrt(squares * (1.0 / 8192) + 1e-05)
    logits = [v * spread for v in logits]

    first, second = ids_ref[0, 0], ids_ref[0, 1]
    zero = jnp.zeros((1, 1), F32)
    logit_a, logit_b = zero, zero
    for e in range(4):
        logit_a = logit_a + jnp.where(first == e, logits[e], zero)
        logit_b = logit_b + jnp.where(second == e, logits[e], zero)
    gate_a = 1.0 / (1.0 + jnp.exp(logit_b - logit_a))
    gate_b = 1.0 / (1.0 + jnp.exp(logit_a - logit_b))
    lane = iota((8, 128), 1)
    gates[...] = (
        jnp.where(lane == first, gate_a, 0.0) + jnp.where(lane == second, gate_b, 0.0)
        + jnp.where(lane == 4, spread, 0.0)
    )
    gate_copies = [
        send(gates.at[pl.ds(0, 1)], gate_in.at[zc, pl.ds(0, 1)], sgate, k, d)
        for k, (p, d) in enumerate(zc_peers)
    ]
    gate_in[zc] = gates[...]
    pending += halves[0] + halves[1] + gate_copies

    def block(part, j, i):
        if part == 0:
            return xa.at[core, (y + 4 - j) % 4, (x + 4 - i) % 4]
        return xb.at[core, (y + 4 - i) % 4, (x + 4 - j) % 4]

    def line(part, i):
        if part == 0:
            return xa.at[core, :, (x + 4 - i) % 4]
        return xb.at[core, (y + 4 - i) % 4]

    first_axis = [[d for _, d in y_peers], [d for _, d in x_peers]]
    second_axis = [[d for _, d in x_peers], [d for _, d in y_peers]]
    across = [[], []]
    middle = [{}, {}]
    onward = [{}, {}]

    def pass_on(part, j):
        ref = block(part, j, 0)
        for to, k in ((0, 0), (2, 4)):
            onward[part][k + j] = send(ref, ref, sg3, part * 12 + k + j, second_axis[part][to])
        if j == 2:
            onward[part][10] = send(ref, ref, sg3, part * 12 + 10, second_axis[part][1])
        if j == 2:
            across[part].append(send(line(part, 0), line(part, 0), sg4, part * 10, sibling))

    def relay(part, j):
        if j % 2 == 0:
            onward[part][j].wait_recv()
            ref, to = block(part, j, 1), second_axis[part][0]
        else:
            onward[part][4 + j].wait_recv()
            ref, to = block(part, j, 3), second_axis[part][2]
        onward[part][8 + j] = send(ref, ref, sg3, part * 12 + 8 + j, to)

    def begin(part):
        for c in halves[part]:
            c.wait_recv()
        g1f[...] = rows(g1r, part, 256)[...].astype(F32)
        ref = block(part, 0, 0)
        for j in range(16):
            ref[:, j * 128 : j * 128 + 128] = g1f[pl.ds(j, 16, stride=16), :].astype(BF16)
        for k in (1, 0, 2):
            middle[part][k] = send(ref, ref, sg2, part * 3 + k, first_axis[part][k])
        pass_on(part, 0)

    def come(part, j):
        middle[part][j - 1].wait_recv()
        pass_on(part, j)

    def lines(part):
        for j in (1, 2, 3):
            onward[part][j].wait_recv()
        across[part].append(send(line(part, 1), line(part, 1), sg4, part * 10 + 4, sibling))
        for j in (0, 2):
            onward[part][4 + j].wait_recv()
        across[part].append(send(line(part, 3), line(part, 3), sg4, part * 10 + 5, sibling))

    def last_line(part):
        for j in (0, 1, 3, 2):
            onward[part][8 + j].wait_recv()
        across[part].append(send(line(part, 2), line(part, 2), sg4, part * 10 + 6, sibling))

    begin(0)
    begin(1)
    for j in (1, 3):
        for part in range(2):
            come(part, j)
    for part in range(2):
        relay(part, 0)
    for part in range(2):
        come(part, 2)
    for j in (1, 3):
        for part in range(2):
            relay(part, j)
    lines(0)
    lines(1)
    for c in gate_copies:
        c.wait_recv()
    for i in range(16):
        gate_all[y, x, i : i + 1] = gate_in[i, 0:1]
    ref = gate_all.at[y, x]
    gate_middle = [send(ref, ref, sgate, 15 + k, d) for k, d in enumerate(first_axis[0])]
    last_line(0)
    last_line(1)
    for c in gate_middle:
        c.wait_recv()
    ref = gate_all.at[:, x]
    gate_onward = [send(ref, ref, sgate, 18 + k, d) for k, d in enumerate(second_axis[0])]
    loads[2].wait()
    loads[3].wait()

    def into(half, part, first=False):
        rows_in = (xa, xb)[part][half].reshape(256, 2048)
        column = pl.ds(pl.multiple_of(half * 4096 + part * 2048, 2048), 2048)
        for k in range(2):
            product = nt(rows_in, w_in[k, :, column])
            acc[k] = product if first else acc[k] + product

    into(core, 0, first=True)
    into(core, 1)
    for c in across[0]:
        c.wait_recv()
    into(1 - core, 0)
    for c in gate_onward:
        c.wait_recv()
    row_facts = gate_all[...].reshape(256, 128)
    lane = iota((256, 128), 1)
    gate = jnp.sum(jnp.where(lane == tier, row_facts, 0.0), axis=1, keepdims=True)
    factor = jnp.sum(jnp.where(lane == 4, row_facts, 0.0), axis=1, keepdims=True)
    for c in across[1]:
        c.wait_recv()
    into(1 - core, 1)
    pending += across[0] + across[1] + gate_middle + gate_onward
    for part in range(2):
        pending += list(middle[part].values()) + list(onward[part].values())

    loads[4].wait()
    gate_part = acc[0] * factor
    act[...] = (gate_part / (1.0 + jnp.exp(-gate_part)) * (acc[1] * factor)).astype(BF16)

    def down(half, part, t):
        column = pl.ds(pl.multiple_of(half * 4096 + part * 2048 + t * TN, TN), TN)
        return nn(act[...], w_down[:, column]) * gate

    chunks = range(4)

    def cut(t):
        return slice(t * TN, t * TN + TN)

    over = {}

    def sibling_chunk(t):
        for part in range(2):
            f0s[part, :, :, :, cut(t)] = down(1 - core, part, t).astype(BF16).reshape(4, 4, 16, TN)
            at = (part, slice(None), slice(None), slice(None), cut(t))
            over[part, t] = send(f0s.at[at], f0r.at[at], sf0, part * 4 + t, sibling)

    def toward(part, t, i):
        if part == 0:
            return f1s.at[0, :, (x + 4 + i) % 4, :, cut(t)]
        return f1s.at[1, (y + 4 + i) % 4, :, :, cut(t)]

    plain, opposite, joined, final = {}, {}, {}, {}

    def way(part, t):
        axis = second_axis[part]
        return (1, axis[0], axis[2]) if t % 2 == 0 else (-1, axis[2], axis[0])

    def own_chunk(t):
        for part in range(2):
            over[part, t].wait_recv()
            both = down(core, part, t) + f0r[part, :, :, :, cut(t)].reshape(256, TN).astype(F32)
            f1s[part, :, :, :, cut(t)] = both.astype(BF16).reshape(4, 4, 16, TN)
            step, ahead, behind = way(part, t)
            k = (part * 4 + t) * 3
            if t == 3:
                axis = second_axis[part]
                at = (part, slice(None), slice(None), cut(t))
                opposite[part, t] = send(toward(part, t, 2), fo.at[at], sf1, k, axis[1])
                plain[part, t] = send(toward(part, t, 1), fd.at[at], sf1, k + 1, axis[0])
                joined[part, t] = send(toward(part, t, 3), fcr.at[at], sf1, k + 2, axis[2])
                continue
            opposite[part, t] = send(toward(part, t, 2), fo.at[part, :, :, cut(t)], sf1, k, ahead)
            plain[part, t] = send(toward(part, t, -step), fd.at[part, :, :, cut(t)], sf1, k + 1, behind)

    def join_chunk(t):
        for part in range(2):
            step, ahead, behind = way(part, t)
            opposite[part, t].wait_recv()
            fcs[part, :, :, cut(t)] = (
                toward(part, t, step)[...].astype(F32) + fo[part, :, :, cut(t)].astype(F32)
            ).astype(BF16)
            at = (part, slice(None), slice(None), cut(t))
            joined[part, t] = send(fcs.at[at], fcr.at[at], sf1, (part * 4 + t) * 3 + 2, ahead)

    def end_chunk(t):
        for part in range(2):
            plain[part, t].wait_recv()
            joined[part, t].wait_recv()
            total = (
                toward(part, t, 0)[...].astype(F32)
                + fd[part, :, :, cut(t)].astype(F32)
                + fcr[part, :, :, cut(t)].astype(F32)
            )
            if t == 3:
                opposite[part, t].wait_recv()
                total = total + fo[part, :, :, cut(t)].astype(F32)
            f2s[part, :, :, cut(t)] = total.astype(BF16)
            for k, (p, d) in enumerate((y_peers, x_peers)[part]):
                final[part, t, k] = send(
                    f2s.at[part, p, :, cut(t)], f2r.at[part, k, :, cut(t)], sf2, (part * 4 + t) * 3 + k, d
                )

    last = {}

    def finish_chunk(t):
        half = t // 2
        for part in range(2):
            for k in range(3):
                final[part, t, k].wait_recv()
            for j in range(4):
                at = slice((t * 4 + j) * 128, (t * 4 + j + 1) * 128)
                total = f2s[part, (y, x)[part], :, at].astype(F32)
                for k in range(3):
                    total = total + f2r[part, k, :, at].astype(F32)
                f3f[pl.ds(half * 256 + part * 8 + t % 2 * 4 + j, 16, stride=16), :] = total
        if t % 2 == 1:
            rows(f3s, half, 256)[...] = rows(f3f, half, 256)[...].astype(BF16)
            for k, (p, d) in enumerate(zc_peers):
                last[half, k] = send(rows(f3s, half * 16 + p, 16), f3r.at[half, zc], sf3, half * 15 + k, d)
            f3r[half, zc] = rows(f3s, half * 16 + zc, 16)[...]

    sibling_chunk(0)
    sibling_chunk(1)
    own_chunk(0)
    sibling_chunk(2)
    own_chunk(1)
    sibling_chunk(3)
    own_chunk(2)
    join_chunk(0)
    own_chunk(3)
    join_chunk(1)
    join_chunk(2)
    end_chunk(0)
    end_chunk(1)
    end_chunk(2)
    finish_chunk(0)
    end_chunk(3)
    finish_chunk(1)
    finish_chunk(2)
    finish_chunk(3)
    for sent in (over, plain, opposite, joined, final, last):
        pending += list(sent.values())
    for c in pending:
        c.wait_send()
    for c in last.values():
        c.wait_recv()
    sums = []
    for c in range(2):
        parts = []
        for half in range(2):
            total = f3r[half, c].astype(F32)
            for k in range(1, 8):
                total = total + f3r[half, 2 * k + c].astype(F32)
            parts.append(total)
        sums += [parts[0][:8], parts[1][:8], parts[0][8:], parts[1][8:]]
    out_ref[...] = (hid[...] + jnp.concatenate(sums, axis=0)).astype(BF16)


def on_device(
    resid, query, fresh_kv, cache_home, kv_cache, cached_len, wo, norm_gain, w_router,
    expert_ids, w_gate, w_up, w_down,
):
    vmem, smem, hbm = (
        pl.BlockSpec(memory_space=pltpu.VMEM),
        pl.BlockSpec(memory_space=pltpu.SMEM),
        pl.BlockSpec(memory_space=pl.ANY),
    )
    v = pltpu.VMEM
    sem = lambda n: pltpu.SemaphoreType.DMA((2, n))
    out = pl.pallas_call(
        kernel,
        out_shape=jax.ShapeDtypeStruct((64, 128), BF16),
        in_specs=[vmem, smem, smem, vmem, vmem] + [hbm] * 8,
        out_specs=vmem,
        scratch_shapes=[
            v((128, 2048), BF16), v((128, 8192), BF16), v((2, 192, 8192), BF16), v((192, 8192), BF16),
            pltpu.SemaphoreType.DMA((8,)),
            v((1, 8192), BF16), v((64, 128), BF16), v((4, 8192), BF16),
            v((128, 128), BF16), v((128, 128), BF16), v((128, 128), F32), v((128, 128), BF16), v((128, 128), BF16),
            v((64, 128), F32), v((64, 128), F32), v((64, 128), F32), v((64, 128), F32),
            v((2, 8, 16, WZ), BF16), v((2, 7, 16, WZ), BF16), v((2, 8, 16, WX), BF16), v((2, 7, 16, WX), BF16),
            v((16 * PZ, 128), BF16), v((2, 7, PZ, 128), BF16), v((16 * PX, 128), BF16), v((2, 7, PX, 128), BF16),
            v((16 * PZ, 128), F32), v((16 * PX, 128), F32), v((64, 128), F32), v((512, 128), F32),
            v((64, 128), BF16), v((512, 128), BF16), v((256, 128), F32),
            v((8, 128), F32), v((16, 8, 128), F32), v((4, 4, 16, 128), F32),
            v((2, 4, 4, 16, 2048), BF16), v((2, 4, 4, 16, 2048), BF16),
            v((2, 256, 192), F32), v((256, 192), BF16),
            v((2, 4, 4, 16, 2048), BF16), v((2, 4, 4, 16, 2048), BF16), v((2, 4, 4, 16, 2048), BF16),
            v((2, 4, 16, 2048), BF16), v((2, 4, 16, 2048), BF16), v((2, 4, 16, 2048), BF16), v((2, 4, 16, 2048), BF16),
            v((2, 4, 16, 2048), BF16), v((2, 3, 16, 2048), BF16),
            v((512, 128), F32), v((512, 128), BF16), v((2, 16, 16, 128), BF16),
            sem(7), sem(7), sem(7), sem(7), sem(14), sem(14), sem(14), sem(14),
            sem(30), sem(21), sem(6), sem(24), sem(20), sem(8), sem(24), sem(24), sem(30),
        ],
        compiler_params=pltpu.CompilerParams(
            collective_id=0, has_side_effects=True, vmem_limit_bytes=60 * 2**20
        ),
    )(
        cache_home, cached_len, expert_ids, query, jnp.transpose(fresh_kv), resid,
        norm_gain.reshape(64, 128), jnp.transpose(w_router),
        kv_cache, wo, w_gate, w_up, w_down,
    )
    return out.reshape(1, 8192)


def solution(mesh):
    return jax.shard_map(
        on_device,
        mesh=mesh,
        in_specs=(
            P(("tier", "grp"), None),
            P("tier", "grp"),
            P("tier", "grp"),
            P("tier", None),
            P(("tier", "grp"), None, None),
            P(("tier", "grp")),
            P("grp", None),
            P(),
            P(),
            P(("tier", "grp"), None),
            P("tier", "grp", None),
            P("tier", "grp", None),
            P("tier", "grp", None),
        ),
        out_specs=P(("tier", "grp"), None),
        check_vma=False,
    )
```
